256 devices in a mesh: dp: 4 (over x), expert: 64 (over y, z, core).
Axes of the slice: x: 4, y: 4, z: 8, core: 2. Of those that a mesh axis runs over, the one named last changes fastest.
Arguments:
- tokens: bfloat16 [16384, 2048], P(('dp', 'expert')), may hold values from -6 to 6
- expert_ids: int32 [16384, 8], P(('dp', 'expert')), may hold values from 0 to 63, all different within a row; in each aligned block of 64 rows (0 to 63, 64 to 127, ...) at most 9 rows name the same one
- gates: float32 [16384, 8], P(('dp', 'expert')), may hold values from 0.1 to 0.5
- cotangent: bfloat16 [16384, 2048], P(('dp', 'expert')), may hold values from -6 to 6
- w_gate: bfloat16 [64, 2048, 768], P('expert'), may hold values from -0.125 to 0.125
- w_up: bfloat16 [64, 2048, 768], P('expert'), may hold values from -0.125 to 0.125
- w_down: bfloat16 [64, 768, 2048], P('expert'), may hold values from -0.21875 to 0.21875
Outputs:
- mixed: bfloat16 [16384, 2048], P(('dp', 'expert'))
- grad_tokens: bfloat16 [16384, 2048], P(('dp', 'expert'))
- grad_weights: bfloat16 [64, 768, 3, 2048], P('expert', 'dp')
The draws below stay inside these ranges and needn't reach their ends.
Inputs may be any that keep to these rules, and one draw needn't show every extreme that they name: `expert_ids`: each token names 8 different experts. Among the tokens of one device (aligned blocks of 64 rows) no expert is named more than 9 times, and in every draw some expert is named exactly 9 times by the tokens of some device.
All inputs are finite; a program needn't handle non-finite values.
Results may differ from the reference program's by a relative error of at most 0.015.
Values may be sent and summed in bfloat16 or wider, within the bound.
A program may use at most 128 MiB of HBM per device.

```python
import math
import jax
import jax.numpy as jnp
import numpy as np
from jax import lax

D = 2048
FF = 768
TOP = 8
TOK_DEV = 64
EXPERTS = 64
CAP = 9
TOKENS = 16384
N_DP = 4
N_EXPERT = 64


def shard_levels(own_key, dims, pieces, least, largest):
    def one(axis_at, blocks):
        draws = jax.random.uniform(jax.random.fold_in(jax.random.fold_in(own_key, 6), axis_at), (blocks,), jnp.float32, least / len(pieces), largest / len(pieces))
        return jnp.repeat(jnp.exp(draws), dims[axis_at] // blocks).reshape((-1,) + (1,) * (len(dims) - axis_at - 1))

    level = one(*pieces[0])
    for cut in pieces[1:]:
        level = level * one(*cut)
    return level


def deal_out(key, own, number, rows, amount, top, bound, lean):
    order = jax.random.permutation(key, amount)
    packed, ordinary = shares(amount, rows * top, bound, lean, True), shares(amount, rows * top, bound, lean, False)
    places = jnp.arange(amount)

    def named(tallies, offset_by):
        used = int((tallies > 0).sum())
        fixed = max(1, used // 4)
        moved = fixed + (places - fixed + offset_by * (used - fixed)) % max(1, amount - fixed)
        return jnp.zeros((amount,), jnp.int32).at[order[jnp.where(places < fixed, places, moved)]].set(jnp.asarray(tallies, jnp.int32))

    tallies = jnp.where(number % 4 == 0, named(packed, number // 4), named(ordinary, number - number // 4 - 1))
    mixed = jax.random.permutation(jax.random.fold_in(own, 3), amount)
    source_of, receiver = mixed[0:amount // 2 * 2:2], mixed[1:amount // 2 * 2:2]
    margin = jnp.minimum(tallies[source_of] - 1, bound - tallies[receiver]) // 2
    margin = jnp.where((source_of == order[0]) | (receiver == order[0]) | (tallies[receiver] == 0), 0, jnp.maximum(margin, 0))
    moved = jax.random.randint(jax.random.fold_in(own, 4), (amount // 2,), 0, 1 << 20) % (margin + 1)
    tallies = tallies.at[source_of].add(-moved).at[receiver].add(moved)
    items = jnp.searchsorted(jnp.cumsum(tallies), jnp.arange(rows * top), side="right").astype(jnp.int32)
    grid = items.reshape(top, rows).T
    grid = grid[jax.random.permutation(jax.random.fold_in(own, 1), rows)]
    offset_by = jax.random.randint(jax.random.fold_in(own, 2), (rows, 1), 0, top)
    return jnp.take_along_axis(grid, (jnp.arange(top)[None, :] + offset_by) % top, axis=1)


def shares(number_of, total, most, slope, full):
    loads = [(1 << 20) // math.isqrt(standing ** slope) + 1 for standing in range(1, number_of + 1)]
    largest = most if full else min(most, max(-(-total // number_of), total * loads[0] // sum(loads)))
    least = 1 if total - largest >= number_of - 1 else 0
    counts, rest = [largest] + [least] * (number_of - 1), total - largest - least * (number_of - 1)
    while rest > 0:
        candidates = [i for i in range(1, number_of) if counts[i] < largest] or [i for i in range(1, number_of) if counts[i] < most]
        pool, left = sum([loads[i] for i in candidates]), rest
        for i in candidates:
            extra = min(most - counts[i], max(1, left * loads[i] // pool), rest)
            counts[i] = counts[i] + extra
            rest = rest - extra
    return np.array(counts)


def normal_values(stream_key, dims, scale, reach, pieces=(), kind=jnp.bfloat16):
    entries = scale * jax.random.normal(stream_key, dims, jnp.float32)
    if pieces:
        entries = entries * shard_levels(stream_key, dims, pieces, -0.22, 0.18)
    return jnp.clip(entries, -reach, reach).astype(kind)


def setup_inputs(seed: int = 0) -> dict:
    splits = jax.random.split(jax.random.key(seed), 8)
    tokens = normal_values(splits[0], (TOKENS, D), 1.0, 6.0, ((0, 256),))
    expert_ids_keys = jax.random.split(jax.random.fold_in(splits[1], 1), TOKENS // TOK_DEV)
    expert_ids_turns = jax.random.permutation(jax.random.fold_in(splits[1], 3), TOKENS // TOK_DEV)
    expert_ids = jax.vmap(lambda own, number: deal_out(jax.random.fold_in(splits[1], 2), own, number, TOK_DEV, EXPERTS, TOP, CAP, 2))(expert_ids_keys, expert_ids_turns).reshape((TOKENS, TOP))
    gates = jnp.clip(0.1 + 0.4 * jax.random.uniform(splits[2], (TOKENS, TOP), jnp.float32) ** shard_levels(splits[2], (TOKENS, TOP), ((0, 256),), -0.2, 0.2), 0.1, 0.5)
    cotangent = normal_values(splits[3], (TOKENS, D), 1.0, 6.0, ((0, 256),))
    w_gate = normal_values(splits[4], (EXPERTS, D, FF), D ** -0.5, 0.125, ((0, 64),))
    w_up = normal_values(splits[5], (EXPERTS, D, FF), D ** -0.5, 0.125, ((0, 64),))
    w_down = normal_values(splits[6], (EXPERTS, FF, D), FF ** -0.5, 0.21875, ((0, 64),))
    return dict(tokens=tokens, expert_ids=expert_ids, gates=gates, cotangent=cotangent, w_gate=w_gate, w_up=w_up, w_down=w_down)


def reference(tokens, expert_ids, gates, cotangent, w_gate, w_up, w_down):
    sources = N_DP * N_EXPERT
    pairs = TOK_DEV * TOP
    rows = sources * CAP
    ids = expert_ids.reshape(sources, pairs)
    onehot = (ids[:, :, None] == jnp.arange(EXPERTS, dtype=jnp.int32)[None, None, :]).astype(jnp.int32)
    slot = jnp.sum((jnp.cumsum(onehot, axis=1) - onehot) * onehot, axis=2)
    row = (jnp.arange(sources, dtype=jnp.int32)[:, None] * CAP + slot).reshape(-1).astype(jnp.int32)
    flat_ids = expert_ids.reshape(-1).astype(jnp.int32)
    repeated = jnp.repeat(tokens, TOP, axis=0)
    routed = (gates[:, :, None] * cotangent[:, None, :].astype(jnp.float32)).astype(jnp.bfloat16).reshape(-1, D)

    def expert_step(index):
        target = jnp.where(flat_ids == index, row, rows).astype(jnp.int32)
        expert_in = jnp.zeros((rows, D), jnp.bfloat16).at[target].set(repeated, mode="drop")
        routed_in = jnp.zeros((rows, D), jnp.bfloat16).at[target].set(routed, mode="drop")
        gate_w = w_gate[index]
        up_w = w_up[index]
        down_w = w_down[index]
        gate_pre = jnp.dot(expert_in, gate_w, preferred_element_type=jnp.float32)
        up_pre = jnp.dot(expert_in, up_w, preferred_element_type=jnp.float32)
        sigma = jax.nn.sigmoid(gate_pre)
        active = gate_pre * sigma
        hidden = (active * up_pre).astype(jnp.bfloat16)
        expert_out = jnp.dot(hidden, down_w, preferred_element_type=jnp.float32).astype(jnp.bfloat16)
        hidden_grad = jnp.dot(routed_in, down_w.T, preferred_element_type=jnp.float32)
        gate_grad = (hidden_grad * up_pre * sigma * (1.0 + gate_pre * (1.0 - sigma))).astype(jnp.bfloat16)
        up_grad = (hidden_grad * active).astype(jnp.bfloat16)
        slot_grad = (jnp.dot(gate_grad, gate_w.T, preferred_element_type=jnp.float32)
                     + jnp.dot(up_grad, up_w.T, preferred_element_type=jnp.float32)).astype(jnp.bfloat16)
        grad_g = jnp.dot(gate_grad.T, expert_in, preferred_element_type=jnp.float32)
        grad_u = jnp.dot(up_grad.T, expert_in, preferred_element_type=jnp.float32)
        grad_d = jnp.dot(hidden.T, routed_in, preferred_element_type=jnp.float32)
        grads = jnp.stack([grad_g, grad_u, grad_d], axis=1).astype(jnp.bfloat16)
        return expert_out, slot_grad, grads

    outputs, slot_grads, grad_weights = lax.map(expert_step, jnp.arange(EXPERTS, dtype=jnp.int32))
    index = (flat_ids * rows + row).astype(jnp.int32)
    picked = outputs.reshape(EXPERTS * rows, D)[index].reshape(TOKENS, TOP, D)
    mixed = jnp.sum(gates[:, :, None] * picked.astype(jnp.float32), axis=1).astype(jnp.bfloat16)
    returned = slot_grads.reshape(EXPERTS * rows, D)[index].reshape(TOKENS, TOP, D)
    grad_tokens = jnp.sum(returned.astype(jnp.float32), axis=1).astype(jnp.bfloat16)
    return mixed, grad_tokens, grad_weights
```

```python
import jax
import jax.numpy as jnp
from jax import lax
from jax.experimental import pallas as pl
from jax.experimental.pallas import tpu as pltpu
from jax.sharding import PartitionSpec as P

MESH = pl.DeviceIdType.MESH
BF = jnp.bfloat16
F32 = jnp.float32

NX, NY, NZ = 4, 4, 8
D, FF, TOK, TOP, CAP = 2048, 768, 64, 8, 9
HALF = D // 2
BLK = 16 * CAP
ROWS = NY * BLK
SHARE = FF // NX
QC = 512
NQ = HALF // QC
ORDER = (2, 6, 4, 3, 7, 5, 1, 0)


def dot(a, b, ca, cb):
    return lax.dot_general(a, b, (((ca,), (cb,)), ((), ())), preferred_element_type=F32)


def kernel(
    tok, cot, ids, gates, wg_h, wu_h, wd_h,
    mixed_o, gtok_o, gw_o,
    T, S, meta_s, meta_r, pos, gat, yb, xin, wg, wu, wd, act, ret, zr, G, xr1, xr2, tw,
    w_sem, tws, twr, tls, ms, mr, zs, zrv, ys, yr, rs, rr, zbs, zbr, xs, xrv, os_, orv, ol,
):
    x = lax.axis_index("dp")
    e = lax.axis_index("expert")
    y, z, c = e // 16, lax.rem(e // 2, NZ), lax.rem(e, 2)

    def at(dx, dy, dz, dc):
        return (
            lax.rem(x + dx + NX, NX),
            (lax.rem(y + dy + NY, NY) * NZ + lax.rem(z + dz + NZ, NZ)) * 2 + lax.rem(c + dc, 2),
        )

    def remote(src, dst, ssem, rsem, where):
        return pltpu.make_async_remote_copy(
            src_ref=src, dst_ref=dst, send_sem=ssem, recv_sem=rsem,
            device_id=where, device_id_type=MESH,
        )

    w_in = [
        pltpu.make_async_copy(src, dst, w_sem.at[i])
        for i, (src, dst) in enumerate(((wg_h, wg), (wu_h, wu), (wd_h, wd)))
    ]
    for cp in w_in:
        cp.start()

    greet = [(0, 0, dz, dc) for dz in range(NZ) for dc in range(2) if dz or dc]
    greet += [(0, dy, 0, dc) for dy in range(1, NY) for dc in range(2)]
    greet += [(1, 0, 0, 0), (-1, 0, 0, 0)]
    bar = pltpu.get_barrier_semaphore()
    for g in greet:
        pl.semaphore_signal(bar, inc=1, device_id=at(*g), device_id_type=MESH)
    pl.semaphore_wait(bar, len(greet))

    def zrow(dz, lo=0, n=128):
        return pl.ds(pl.multiple_of(lax.rem(z + dz + NZ, NZ) * 128 + lo, 16), n)

    mine = pl.ds(pl.multiple_of(c * HALF, HALF), HALF)
    other = pl.ds(pl.multiple_of((1 - c) * HALF, HALF), HALF)

    swaps, keeps = [], []
    for a, src in enumerate((tok, cot)):
        rows = pl.ds(pl.multiple_of(z * 128 + c * TOK, TOK), TOK)
        cp = remote(src.at[:, other], T.at[a, rows, :], tws.at[a], twr.at[a], at(0, 0, 0, 1))
        cp.start()
        swaps.append(cp)
        cp = pltpu.make_async_copy(src.at[:, mine], T.at[a, rows, :], tls.at[a])
        cp.start()
        keeps.append(cp)

    idv = ids[...]
    place = ((idv >> 1) & 7) * 8 + (idv >> 4) * 2 + (idv & 1)
    lane = lax.broadcasted_iota(jnp.int32, (TOK, 64), 1)
    named = jnp.zeros((TOK, 64), F32)
    gated = jnp.zeros((TOK, 64), F32)
    for k in range(TOP):
        hit = place[:, k : k + 1] == lane
        named = named + jnp.where(hit, 1.0, 0.0)
        gated = gated + jnp.where(hit, gates[:, k : k + 1], 0.0)
    t0 = lax.broadcasted_iota(jnp.int32, (TOK, 128), 0)
    l0 = lax.broadcasted_iota(jnp.int32, (TOK, 128), 1) - TOK * c
    same = jnp.where(t0 == l0, 1.0, 0.0).astype(BF)
    upto = jnp.where(t0 <= l0, jnp.where(l0 < TOK, 1.0, 0.0), 0.0).astype(BF)
    named = named.astype(BF)
    rank = dot(named, upto, 0, 0) * dot(named, same, 0, 0)
    gate_t = dot(gated.astype(BF), same, 0, 0)
    for k in range(NZ):
        meta_s[k, 0:8, :] = rank[k * 8 : k * 8 + 8]
        meta_s[k, 8:16, :] = gate_t[k * 8 : k * 8 + 8]
    metas = []
    for dz in (1, 7, 2, 6, 3, 5, 4, 0):
        for dc in (0, 1):
            src = meta_s.at[lax.rem(z + dz, NZ)]
            dst = meta_r.at[z * 2 + c]
            if dz == 0 and dc == 0:
                cp = pltpu.make_async_copy(src, dst, mr.at[0, 0])
            else:
                cp = remote(src, dst, ms.at[dz, dc], mr.at[dz, dc], at(0, 0, dz, dc))
            cp.start()
            metas.append((cp, dz or dc))

    def zcopy(p, q, s, way):
        a = p // NQ
        cols = pl.ds((p % NQ) * QC + q * (QC // 2), QC // 2)
        rows = zrow(-s * way) if s < 3 else zrow(-3 * way, 0 if way == 1 else 64, 64)
        i = 0 if way == 1 else 1
        return remote(
            T.at[a, rows, cols], T.at[a, rows, cols],
            zs.at[p, q, s, i], zrv.at[p, q, s, i], at(0, 0, way, 0),
        )

    zc = {
        (p, q, s, w): zcopy(p, q, s, w)
        for p in range(2 * NQ) for q in range(2) for s in range(4) for w in (1, -1)
    }

    def zstart(p, s):
        for q in range(2):
            for w in (1, -1):
                if s:
                    zc[p, q, s - 1, w].wait_recv()
                zc[p, q, s, w].start()

    def target(r):
        return at(0, r // 2, 0, r % 2)

    my_rows = pl.ds(pl.multiple_of(y * BLK, 16), BLK)

    def ycopy(p, r):
        a, q = p // NQ, p % NQ
        src = yb.at[a, pl.ds(r * BLK, BLK), pl.ds(q * QC, QC)]
        dst = xin.at[a, my_rows, pl.ds(pl.multiple_of(c * HALF + q * QC, QC), QC)]
        if r == 0:
            return pltpu.make_async_copy(src, dst, yr.at[p, 0])
        return remote(src, dst, ys.at[p, r], yr.at[p, r], target(r))

    yc = {(p, r): ycopy(p, r) for p in range(2 * NQ) for r in range(8)}

    def select(p, r):
        a, q = p // NQ, p % NQ
        rows = dot(S[a, r * BLK : (r + 1) * BLK, :], T[a, :, q * QC : (q + 1) * QC], 1, 0)
        yb[a, r * BLK : (r + 1) * BLK, q * QC : (q + 1) * QC] = rows.astype(BF)
        yc[p, r].start()

    for a in range(2):
        swaps[a].wait_recv()
        keeps[a].wait()
    zstart(0, 0)

    for cp, far in metas:
        if far:
            cp.wait_recv()
        else:
            cp.wait()
    lane8 = lax.broadcasted_iota(jnp.int32, (8, 128), 1)
    for k in range(NZ):
        enc = meta_r[2 * k, 0:8, :] + meta_r[2 * k + 1, 0:8, :]
        base = jnp.where(lane8 < TOK, 2.0 * k * CAP - 1.0, (2.0 * k + 1.0) * CAP - 1.0)
        pos[:, k * 128 : (k + 1) * 128] = jnp.where(enc > 0.5, enc + base, -1.0)
        gat[:, k * 128 : (k + 1) * 128] = meta_r[2 * k, 8:16, :] + meta_r[2 * k + 1, 8:16, :]
    zstart(0, 1)
    row16 = lax.broadcasted_iota(jnp.int32, (16, 16 * TOK), 0).astype(F32)

    def build(r, carry):
        j = lax.rem(y + r // 2, NY) * 2 + lax.rem(c + r, 2)
        prow = pos[pl.ds(j, 1), :]
        grow = gat[pl.ds(j, 1), :]
        for i in range(BLK // 16):
            hit = row16 + float(16 * i) == prow
            at_rows = pl.ds(pl.multiple_of(r * BLK + 16 * i, 16), 16)
            S[0, at_rows, :] = jnp.where(hit, 1.0, 0.0).astype(BF)
            S[1, at_rows, :] = jnp.where(hit, grow, 0.0).astype(BF)
        return carry

    lax.fori_loop(0, 8, build, 0)

    NP = 2 * NQ
    for p in range(NP + 1):
        for s in range(4):
            if p < NP and s >= (2 if p == 0 else 1):
                zstart(p, s)
            if s == 3 and p + 1 < NP:
                zstart(p + 1, 0)
            if p:
                for r in ORDER[2 * s : 2 * s + 2]:
                    select(p - 1, r)
        if p < NP:
            for q in range(2):
                for w in (1, -1):
                    zc[p, q, 3, w].wait_recv()

    def arrived(a):
        for p in range(a * NQ, a * NQ + NQ):
            for r in range(8):
                if r:
                    yc[p, r].wait_recv()
                    yc[p, r].wait_send()
                else:
                    yc[p, r].wait()

    arrived(0)
    for cp in w_in:
        cp.wait()
    HR = ROWS // 2

    def forward(i, carry):
        rows = pl.ds(pl.multiple_of(lax.rem(i, 2) * HR, 16), HR)
        cols = pl.ds(pl.multiple_of((i // 2) * 256, 256), 256)
        v = xin[0, rows, :]
        g = dot(v, wg[:, cols], 1, 0)
        u = dot(v, wu[:, cols], 1, 0)
        sg = jax.nn.sigmoid(g)
        silu = g * sg
        act[0, rows, cols] = (silu * u).astype(BF)
        act[1, rows, cols] = (u * sg * (1.0 + g * (1.0 - sg))).astype(BF)
        act[2, rows, cols] = silu.astype(BF)
        return carry

    lax.fori_loop(0, 2 * FF // 256, forward, 0)

    def give_back(a, q, h, rows):
        for k in range(NY):
            r = lax.rem(k - y + NY, NY) * 2 + lax.rem(h - c + 2, 2)
            yb[a, pl.ds(pl.multiple_of(r * BLK, 16), BLK), q * QC : (q + 1) * QC] = (
                rows[k * BLK : (k + 1) * BLK].astype(BF)
            )

    def rcopy(a, q, r):
        cols = pl.ds(q * QC, QC)
        there = (NY - r // 2) % NY * 2 + r % 2
        src = yb.at[a, pl.ds(r * BLK, BLK), cols]
        dst = ret.at[a, pl.ds(there * BLK, BLK), cols]
        if r == 0:
            return pltpu.make_async_copy(src, dst, rr.at[a, q, 0])
        return remote(src, dst, rs.at[a, q, r], rr.at[a, q, r], target(r))

    rc = {(a, q, r): rcopy(a, q, r) for a in range(2) for q in range(NQ) for r in range(8)}

    for q in range(NQ):
        for h in range(2):
            n = h * HALF + q * QC
            give_back(0, q, h, dot(act[0], wd[:, n : n + QC], 1, 0))

    def xshare(dx):
        return lax.rem(x + dx + NX, NX)

    SH2 = SHARE // 2

    def xcopy1(m, way):
        i = 0 if way == 1 else 1
        return remote(
            G.at[xshare(2), m, pl.ds(i * SH2, SH2), :], xr1.at[i, m],
            xs.at[0, m, i], xrv.at[0, m, i], at(way, 0, 0, 0),
        )

    def xcopy2(m, way):
        i = 0 if way == 1 else 1
        return remote(
            G.at[xshare(way), m], xr2.at[i, m],
            xs.at[1, m, i], xrv.at[1, m, i], at(way, 0, 0, 0),
        )

    xc1 = {(m, w): xcopy1(m, w) for m in range(3) for w in (1, -1)}
    xc2 = {(m, w): xcopy2(m, w) for m in range(3) for w in (1, -1)}

    def weights(m, b, k):
        def part(i, carry):
            cols = pl.ds(pl.multiple_of(i * QC, QC), QC)
            for hf in range(2):
                v = dot(act[k, :, hf * 384 : (hf + 1) * 384], xin[b, :, cols], 0, 0).astype(BF)
                G[2 * hf, m, :, cols] = v[:SHARE]
                G[2 * hf + 1, m, :, cols] = v[SHARE:]
            return carry

        lax.fori_loop(0, D // QC, part, 0)
        for w in (1, -1):
            xc1[m, w].start()

    arrived(1)
    for q in range(NQ):
        for r in ORDER:
            rc[0, q, r].start()
    weights(2, 1, 0)

    def backward(i, carry):
        cols = pl.ds(pl.multiple_of(i * 256, 256), 256)
        g = dot(xin[1], wd[cols, :], 1, 1)
        act[1, :, cols] = (g * act[1, :, cols].astype(F32)).astype(BF)
        act[2, :, cols] = (g * act[2, :, cols].astype(F32)).astype(BF)
        return carry

    lax.fori_loop(0, FF // 256, backward, 0)
    weights(0, 0, 1)
    weights(1, 0, 2)
    for q in range(NQ):
        for h in range(2):
            n = h * HALF + q * QC
            give_back(
                1, q, h,
                dot(act[1], wg[n : n + QC, :], 1, 1) + dot(act[2], wu[n : n + QC, :], 1, 1),
            )
        for r in ORDER:
            rc[1, q, r].start()

    def xadd(m):
        for i, w in enumerate((1, -1)):
            xc1[m, w].wait_recv()
            rows = pl.ds(i * SH2, SH2)
            d = xshare(w)
            G[d, m, rows, :] = (G[d, m, rows, :].astype(F32) + xr1[i, m].astype(F32)).astype(BF)
            xc2[m, w].start()

    for a in range(2):
        swaps[a].wait_send()
    for key in zc:
        zc[key].wait_send()

    def bcopy(a, q, s, way):
        i = 0 if way == 1 else 1
        cols = pl.ds(q * QC, QC)
        rows = zrow((4 - s) * way) if s else zrow(4, 64 * i, 64)
        dst = zr.at[a, i, s, :, cols] if s else zr.at[a, i, 0, pl.ds(0, 64), cols]
        return remote(
            T.at[a, rows, cols], dst, zbs.at[a, q, s, i], zbr.at[a, q, s, i], at(0, 0, way, 0)
        )

    def combine(a, q):
        for r in range(8):
            if r:
                rc[a, q, r].wait_recv()
            else:
                rc[a, q, r].wait()
        cols = slice(q * QC, (q + 1) * QC)
        for k in range(NZ):
            v = dot(S[1 - a, :, k * 128 : (k + 1) * 128], ret[a, :, cols], 0, 0)
            T[a, k * 128 : (k + 1) * 128, cols] = v.astype(BF)
        done = []
        for s in range(4):
            for i, w in enumerate((1, -1)):
                if s:
                    done[2 * (s - 1) + i].wait_recv()
                    n = 64 if s == 1 else 128
                    rows = zrow((4 - s) * w, 64 * i if s == 1 else 0, n)
                    T[a, rows, cols] = (
                        T[a, rows, cols].astype(F32) + zr[a, i, s - 1, 0:n, cols].astype(F32)
                    ).astype(BF)
                cp = bcopy(a, q, s, w)
                cp.start()
                done.append(cp)
        return done

    def finish(a, q, done):
        cols = slice(q * QC, (q + 1) * QC)
        for cp in done[6:]:
            cp.wait_recv()
        rows = zrow(0)
        T[a, rows, cols] = (
            T[a, rows, cols].astype(F32)
            + zr[a, 0, 3, :, cols].astype(F32)
            + zr[a, 1, 3, :, cols].astype(F32)
        ).astype(BF)

    outs = (mixed_o, gtok_o)
    tail = []

    def hand_over(a):
        theirs = pl.ds(pl.multiple_of(z * 128 + (1 - c) * TOK, TOK), TOK)
        ours = pl.ds(pl.multiple_of(z * 128 + c * TOK, TOK), TOK)
        cp = remote(T.at[a, theirs, :], tw.at[a], os_.at[a], orv.at[a], at(0, 0, 0, 1))
        cp.start()
        keep = pltpu.make_async_copy(T.at[a, ours, :], outs[a].at[:, mine], ol.at[a])
        keep.start()
        return cp, keep

    def take_over(a, pair):
        cp, keep = pair
        cp.wait_recv()
        last = pltpu.make_async_copy(tw.at[a], outs[a].at[:, other], ol.at[2 + a])
        last.start()
        tail.extend((keep, last))

    sent = []
    xadd(2)
    d00 = combine(0, 0)
    xadd(0)
    d01 = combine(0, 1)
    finish(0, 0, d00)
    xadd(1)
    finish(0, 1, d01)
    pair0 = hand_over(0)
    d10 = combine(1, 0)
    take_over(0, pair0)
    d11 = combine(1, 1)
    finish(1, 0, d10)
    finish(1, 1, d11)
    pair1 = hand_over(1)
    take_over(1, pair1)
    for m in (2, 0, 1):
        for w in (1, -1):
            xc2[m, w].wait_recv()
        own = xshare(0)
        G[own, m] = (
            G[own, m].astype(F32) + xr2[0, m].astype(F32) + xr2[1, m].astype(F32)
        ).astype(BF)
        cp = pltpu.make_async_copy(G.at[own, m], gw_o.at[m], ol.at[4 + m])
        cp.start()
        tail.append(cp)

    for cp, far in metas:
        if far:
            cp.wait_send()
    for a in range(2):
        for q in range(NQ):
            for r in range(1, 8):
                rc[a, q, r].wait_send()
    for d in (d00, d01, d10, d11):
        for cp in d:
            cp.wait_send()
    for pair in (pair0, pair1):
        pair[0].wait_send()
    for m in range(3):
        for w in (1, -1):
            xc1[m, w].wait_send()
            xc2[m, w].wait_send()
    for cp in tail:
        cp.wait()


def local(tokens, expert_ids, gates, cotangent, w_gate, w_up, w_down):
    vmem = pl.BlockSpec(memory_space=pltpu.VMEM)
    hbm = pl.BlockSpec(memory_space=pl.ANY)
    dma = pltpu.SemaphoreType.DMA
    mixed, grad_tokens, grads = pl.pallas_call(
        kernel,
        out_shape=(
            jax.ShapeDtypeStruct((TOK, D), BF),
            jax.ShapeDtypeStruct((TOK, D), BF),
            jax.ShapeDtypeStruct((3, SHARE, D), BF),
        ),
        in_specs=[vmem] * 4 + [hbm] * 3,
        out_specs=(hbm, hbm, hbm),
        scratch_shapes=[
            pltpu.VMEM((2, 16 * TOK, HALF), BF),
            pltpu.VMEM((2, 8 * BLK, 16 * TOK), BF),
            pltpu.VMEM((NZ, 16, 128), F32),
            pltpu.VMEM((2 * NZ, 16, 128), F32),
            pltpu.VMEM((8, 16 * TOK), F32),
            pltpu.VMEM((8, 16 * TOK), F32),
            pltpu.VMEM((2, 8 * BLK, HALF), BF),
            pltpu.VMEM((2, ROWS, D), BF),
            pltpu.VMEM((D, FF), BF),
            pltpu.VMEM((D, FF), BF),
            pltpu.VMEM((FF, D), BF),
            pltpu.VMEM((3, ROWS, FF), BF),
            pltpu.VMEM((2, 8 * BLK, HALF), BF),
            pltpu.VMEM((2, 2, 4, 128, HALF), BF),
            pltpu.VMEM((NX, 3, SHARE, D), BF),
            pltpu.VMEM((2, 3, SHARE // 2, D), BF),
            pltpu.VMEM((2, 3, SHARE, D), BF),
            pltpu.VMEM((2, TOK, HALF), BF),
            dma((3,)), dma((2,)), dma((2,)), dma((2,)),
            dma((NZ, 2)), dma((NZ, 2)),
            dma((2 * NQ, 2, 4, 2)), dma((2 * NQ, 2, 4, 2)),
            dma((2 * NQ, 8)), dma((2 * NQ, 8)),
            dma((2, NQ, 8)), dma((2, NQ, 8)),
            dma((2, NQ, 4, 2)), dma((2, NQ, 4, 2)),
            dma((2, 3, 2)), dma((2, 3, 2)),
            dma((2,)), dma((2,)), dma((7,)),
        ],
        compiler_params=pltpu.CompilerParams(
            collective_id=0, has_side_effects=True, vmem_limit_bytes=60 * 2**20
        ),
        cost_estimate=pl.CostEstimate(
            flops=30_000_000_000, bytes_accessed=20_000_000, transcendentals=450_000
        ),
        name="moe",
    )(tokens, cotangent, expert_ids, gates, w_gate[0], w_up[0], w_down[0])
    return mixed, grad_tokens, grads.transpose(1, 0, 2)[None]


def solution(mesh):
    return jax.shard_map(
        local,
        mesh=mesh,
        in_specs=(
            P(("dp", "expert"), None),
            P(("dp", "expert"), None),
            P(("dp", "expert"), None),
            P(("dp", "expert"), None),
            P("expert", None, None),
            P("expert", None, None),
            P("expert", None, None),
        ),
        out_specs=(
            P(("dp", "expert"), None),
            P(("dp", "expert"), None),
            P("expert", "dp", None, None),
        ),
        check_vma=False,
    )
```

```python
import jax
import jax.numpy as jnp
from jax import lax
from jax.experimental import pallas as pl
from jax.experimental.pallas import tpu as pltpu
from jax.sharding import PartitionSpec as P

MESH = pl.DeviceIdType.MESH
BF = jnp.bfloat16
F32 = jnp.float32

NX, NY, NZ = 4, 4, 8
D, FF, TOK, TOP, CAP = 2048, 768, 64, 8, 9
HALF = D // 2
BLK = 16 * CAP
ROWS = NY * BLK
SHARE = FF // NX
QC = 256
NQ = HALF // QC
WIDE = 512
ORDER = (2, 6, 4, 3, 7, 5, 1, 0)


def dot(a, b, ca, cb):
    return lax.dot_general(a, b, (((ca,), (cb,)), ((), ())), preferred_element_type=F32)


def kernel(
    tok, cot, ids, gates, wg_h, wu_h, wd_h,
    mixed_o, gtok_o, gw_o,
    T, S, meta_s, meta_r, pos, gat, yb, xin, wg, wu, wd, act, ret, zr, G, xr1, xr2, tw,
    w_sem, tws, twr, tls, ms, mr, zs, zrv, ys, yr, rs, rr, zbs, zbr, xs, xrv, os_, orv, ol,
):
    x = lax.axis_index("dp")
    e = lax.axis_index("expert")
    y, z, c = e // 16, lax.rem(e // 2, NZ), lax.rem(e, 2)

    def at(dx, dy, dz, dc):
        return (
            lax.rem(x + dx + NX, NX),
            (lax.rem(y + dy + NY, NY) * NZ + lax.rem(z + dz + NZ, NZ)) * 2 + lax.rem(c + dc, 2),
        )

    def remote(src, dst, ssem, rsem, where):
        return pltpu.make_async_remote_copy(
            src_ref=src, dst_ref=dst, send_sem=ssem, recv_sem=rsem,
            device_id=where, device_id_type=MESH,
        )

    w_in = [
        pltpu.make_async_copy(src, dst, w_sem.at[i])
        for i, (src, dst) in enumerate(((wg_h, wg), (wu_h, wu), (wd_h, wd)))
    ]
    for cp in w_in:
        cp.start()

    idv = ids[...]
    place = ((idv >> 1) & 7) * 8 + (idv >> 4) * 2 + (idv & 1)
    row = lax.broadcasted_iota(jnp.int32, (64, TOK), 0)
    named = jnp.zeros((64, TOK), F32)
    gated = jnp.zeros((64, TOK), F32)
    for k in range(TOP):
        hit = place[k : k + 1, :] == row
        named = named + jnp.where(hit, 1.0, 0.0)
        gated = gated + jnp.where(hit, gates[k : k + 1, :], 0.0)
    t0 = lax.broadcasted_iota(jnp.int32, (TOK, 128), 0)
    l0 = lax.broadcasted_iota(jnp.int32, (TOK, 128), 1) - TOK * c
    same = jnp.where(t0 == l0, 1.0, 0.0).astype(BF)
    upto = jnp.where(t0 <= l0, jnp.where(l0 < TOK, 1.0, 0.0), 0.0).astype(BF)
    named = named.astype(BF)
    rank = dot(named, upto, 1, 0) * dot(named, same, 1, 0)
    gate_t = dot(gated.astype(BF), same, 1, 0)
    for k in range(NZ):
        meta_s[k, 0:8, :] = rank[k * 8 : k * 8 + 8]
        meta_s[k, 8:16, :] = gate_t[k * 8 : k * 8 + 8]

    greet = [(0, 0, dz, dc) for dz in range(NZ) for dc in range(2) if dz or dc]
    greet += [(0, dy, 0, dc) for dy in range(1, NY) for dc in range(2)]
    greet += [(1, 0, 0, 0), (-1, 0, 0, 0)]
    bar = pltpu.get_barrier_semaphore()
    for g in greet:
        pl.semaphore_signal(bar, inc=1, device_id=at(*g), device_id_type=MESH)
    pl.semaphore_wait(bar, len(greet))

    def zrow(dz, lo=0, n=128):
        return pl.ds(pl.multiple_of(lax.rem(z + dz + NZ, NZ) * 128 + lo, 16), n)

    mine = pl.ds(pl.multiple_of(c * HALF, HALF), HALF)
    other = pl.ds(pl.multiple_of((1 - c) * HALF, HALF), HALF)

    swaps, keeps = [], []
    for a, src in enumerate((tok, cot)):
        rows = pl.ds(pl.multiple_of(z * 128 + c * TOK, TOK), TOK)
        cp = remote(src.at[:, other], T.at[a, rows, :], tws.at[a], twr.at[a], at(0, 0, 0, 1))
        cp.start()
        swaps.append(cp)
        cp = pltpu.make_async_copy(src.at[:, mine], T.at[a, rows, :], tls.at[a])
        cp.start()
        keeps.append(cp)

    metas = []
    for dz in (1, 7, 2, 6, 3, 5, 4, 0):
        for dc in (0, 1):
            src = meta_s.at[lax.rem(z + dz, NZ)]
            dst = meta_r.at[z * 2 + c]
            if dz == 0 and dc == 0:
                cp = pltpu.make_async_copy(src, dst, mr.at[0, 0])
            else:
                cp = remote(src, dst, ms.at[dz, dc], mr.at[dz, dc], at(0, 0, dz, dc))
            cp.start()
            metas.append((cp, dz or dc))

    NP = 2 * NQ

    def zcopy(p, s, way):
        a = p // NQ
        cols = pl.ds((p % NQ) * QC, QC)
        rows = zrow(-s * way) if s < 3 else zrow(-3 * way, 0 if way == 1 else 64, 64)
        i = 0 if way == 1 else 1
        return remote(
            T.at[a, rows, cols], T.at[a, rows, cols],
            zs.at[p, s, i], zrv.at[p, s, i], at(0, 0, way, 0),
        )

    zc = {(p, s, w): zcopy(p, s, w) for p in range(NP) for s in range(4) for w in (1, -1)}

    def zstart(p, s):
        for w in (1, -1):
            if s:
                zc[p, s - 1, w].wait_recv()
            zc[p, s, w].start()

    def target(r):
        return at(0, r // 2, 0, r % 2)

    my_rows = pl.ds(pl.multiple_of(y * BLK, 16), BLK)

    def ycopy(p, r):
        a, q = p // NQ, p % NQ
        src = yb.at[a, pl.ds(r * BLK, BLK), pl.ds(q * QC, QC)]
        dst = xin.at[a, my_rows, pl.ds(pl.multiple_of(c * HALF + q * QC, QC), QC)]
        if r == 0:
            return pltpu.make_async_copy(src, dst, yr.at[p, 0])
        return remote(src, dst, ys.at[p, r], yr.at[p, r], target(r))

    yc = {(p, r): ycopy(p, r) for p in range(NP) for r in range(8)}

    def select(p, dy):
        a, q = p // NQ, p % NQ
        block = slice(2 * dy * BLK, 2 * (dy + 1) * BLK)
        cols = slice(q * QC, (q + 1) * QC)
        yb[a, block, cols] = dot(S[a, block, :], T[a, :, cols], 1, 0).astype(BF)
        yc[p, 2 * dy + 1].start()
        yc[p, 2 * dy].start()

    for a in range(2):
        swaps[a].wait_recv()
        keeps[a].wait()
    zstart(0, 0)
    zstart(0, 1)
    zstart(1, 0)

    for cp, far in metas:
        if far:
            cp.wait_recv()
        else:
            cp.wait()
    lane8 = lax.broadcasted_iota(jnp.int32, (8, 128), 1)
    for k in range(NZ):
        enc = meta_r[2 * k, 0:8, :] + meta_r[2 * k + 1, 0:8, :]
        base = jnp.where(lane8 < TOK, 2.0 * k * CAP - 1.0, (2.0 * k + 1.0) * CAP - 1.0)
        pos[:, k * 128 : (k + 1) * 128] = jnp.where(enc > 0.5, enc + base, -1.0)
        gat[:, k * 128 : (k + 1) * 128] = meta_r[2 * k, 8:16, :] + meta_r[2 * k + 1, 8:16, :]
    row16 = lax.broadcasted_iota(jnp.int32, (16, 16 * TOK), 0).astype(F32)

    def build(r, carry):
        j = lax.rem(y + r // 2, NY) * 2 + lax.rem(c + r, 2)
        prow = pos[pl.ds(j, 1), :]
        grow = gat[pl.ds(j, 1), :]
        for i in range(BLK // 16):
            hit = row16 + float(16 * i) == prow
            at_rows = pl.ds(pl.multiple_of(r * BLK + 16 * i, 16), 16)
            S[0, at_rows, :] = jnp.where(hit, 1.0, 0.0).astype(BF)
            S[1, at_rows, :] = jnp.where(hit, grow, 0.0).astype(BF)
        return carry

    lax.fori_loop(0, 8, build, 0)

    def arrived(p):
        for r in range(8):
            if r:
                yc[p, r].wait_recv()
                yc[p, r].wait_send()
            else:
                yc[p, r].wait()

    HR = ROWS // 2

    def forward(n):
        def part(i, carry):
            rows = pl.ds(pl.multiple_of(i * HR, 16), HR)
            cols = slice(n * 256, (n + 1) * 256)
            v = xin[0, rows, :]
            g = dot(v, wg[:, cols], 1, 0)
            u = dot(v, wu[:, cols], 1, 0)
            sg = jax.nn.sigmoid(g)
            silu = g * sg
            act[0, rows, cols] = (silu * u).astype(BF)
            act[1, rows, cols] = (u * sg * (1.0 + g * (1.0 - sg))).astype(BF)
            act[2, rows, cols] = silu.astype(BF)
            return carry

        lax.fori_loop(0, 2, part, 0)

    DY = (1, 3, 2, 0)
    for t in range(2, NP + 4):
        for i in range(4):
            k = t - 3 + i
            if 0 <= k < NP:
                zstart(k, t - k)
            if i == 0 and t >= 4:
                for w in (1, -1):
                    zc[t - 4, 3, w].wait_recv()
            if t >= 4:
                select(t - 4, DY[i])
        if t == NP:
            for p in range(NQ):
                arrived(p)
            for cp in w_in:
                cp.wait()
        if NP <= t < NP + FF // 256:
            forward(t - NP)

    def give_back(a, q, h, rows):
        for k in range(NY):
            r = lax.rem(k - y + NY, NY) * 2 + lax.rem(h - c + 2, 2)
            yb[a, pl.ds(pl.multiple_of(r * BLK, 16), BLK), q * WIDE : (q + 1) * WIDE] = (
                rows[k * BLK : (k + 1) * BLK].astype(BF)
            )

    def rcopy(a, q, r):
        cols = pl.ds(q * QC, QC)
        there = (NY - r // 2) % NY * 2 + r % 2
        src = yb.at[a, pl.ds(r * BLK, BLK), cols]
        dst = ret.at[a, pl.ds(there * BLK, BLK), cols]
        if r == 0:
            return pltpu.make_async_copy(src, dst, rr.at[a, q, 0])
        return remote(src, dst, rs.at[a, q, r], rr.at[a, q, r], target(r))

    rc = {(a, q, r): rcopy(a, q, r) for a in range(2) for q in range(NQ) for r in range(8)}

    NW = WIDE // QC
    for q in range(HALF // WIDE):
        for h in range(2):
            n = h * HALF + q * WIDE
            give_back(0, q, h, dot(act[0], wd[:, n : n + WIDE], 1, 0))
        for i in range(q * NW, (q + 1) * NW):
            for r in ORDER:
                rc[0, i, r].start()

    def xshare(dx):
        return lax.rem(x + dx + NX, NX)

    SH2 = SHARE // 2

    def piece(n):
        if n < 2:
            return n, slice(0, HALF)
        return 2, slice((n - 2) * QC, (n - 1) * QC)

    PIECES = 2 + NQ

    def xcopy1(n, way):
        i = 0 if way == 1 else 1
        m, cols = piece(n)
        return remote(
            G.at[xshare(2), m, :, pl.ds(i * SH2, SH2), cols], xr1.at[i, m, :, :, cols],
            xs.at[0, n, i], xrv.at[0, n, i], at(way, 0, 0, 0),
        )

    def xcopy2(n, way):
        i = 0 if way == 1 else 1
        m, cols = piece(n)
        return remote(
            G.at[xshare(way), m, :, :, cols], xr2.at[i, m, :, :, cols],
            xs.at[1, n, i], xrv.at[1, n, i], at(way, 0, 0, 0),
        )

    xc1 = {(n, w): xcopy1(n, w) for n in range(PIECES) for w in (1, -1)}
    xc2 = {(n, w): xcopy2(n, w) for n in range(PIECES) for w in (1, -1)}

    def product(m, b, k, h, cols, at_cols):
        for hf in range(2):
            v = dot(act[k, :, hf * 384 : (hf + 1) * 384], xin[b, :, cols], 0, 0).astype(BF)
            G[2 * hf, m, h, :, at_cols] = v[:SHARE]
            G[2 * hf + 1, m, h, :, at_cols] = v[SHARE:]

    def weights(m, b, k):
        def part(i, carry):
            here = pl.ds(pl.multiple_of(i * WIDE, WIDE), WIDE)
            for h in range(2):
                cols = pl.ds(pl.multiple_of(h * HALF + i * WIDE, WIDE), WIDE)
                product(m, b, k, h, cols, here)
            return carry

        lax.fori_loop(0, HALF // WIDE, part, 0)
        for w in (1, -1):
            xc1[m, w].start()

    def xadd(n):
        m, cols = piece(n)
        for i, w in enumerate((1, -1)):
            xc1[n, w].wait_recv()
            rows = pl.ds(i * SH2, SH2)
            d = xshare(w)
            for h in range(2):
                G[d, m, h, rows, cols] = (
                    G[d, m, h, rows, cols].astype(F32) + xr1[i, m, h, :, cols].astype(F32)
                ).astype(BF)
            xc2[n, w].start()

    def xfinish(m):
        for n in range(PIECES):
            if piece(n)[0] == m:
                for w in (1, -1):
                    xc2[n, w].wait_recv()
        own = xshare(0)
        for h in range(2):
            G[own, m, h] = (
                G[own, m, h].astype(F32) + xr2[0, m, h].astype(F32) + xr2[1, m, h].astype(F32)
            ).astype(BF)
            cp = pltpu.make_async_copy(
                G.at[own, m, h], gw_o.at[m, :, pl.ds(h * HALF, HALF)], ol.at[4 + 2 * m + h]
            )
            cp.start()
            tail.append(cp)

    tail = []
    for i in range(NQ):
        arrived(NQ + i)
        for h in range(2):
            n = h * HALF + i * QC
            product(2, 1, 0, h, slice(n, n + QC), slice(i * QC, (i + 1) * QC))
        for w in (1, -1):
            xc1[2 + i, w].start()
        if i:
            xadd(1 + i)

    def backward(i, carry):
        cols = pl.ds(pl.multiple_of(i * 256, 256), 256)
        g = dot(xin[1], wd[cols, :], 1, 1)
        act[1, :, cols] = (g * act[1, :, cols].astype(F32)).astype(BF)
        act[2, :, cols] = (g * act[2, :, cols].astype(F32)).astype(BF)
        return carry

    lax.fori_loop(0, FF // 256, backward, 0)
    weights(0, 0, 1)
    weights(1, 0, 2)
    xadd(1 + NQ)
    for q in range(HALF // WIDE):
        for h in range(2):
            n = h * HALF + q * WIDE
            give_back(
                1, q, h,
                dot(act[1], wg[n : n + WIDE, :], 1, 1) + dot(act[2], wu[n : n + WIDE, :], 1, 1),
            )
        for i in range(q * NW, (q + 1) * NW):
            for r in ORDER:
                rc[1, i, r].start()

    for a in range(2):
        swaps[a].wait_send()
    for key in zc:
        zc[key].wait_send()

    def bcopy(k, s, way):
        a, q = k // NQ, k % NQ
        i = 0 if way == 1 else 1
        cols = pl.ds(q * QC, QC)
        rows = zrow((4 - s) * way) if s else zrow(4, 64 * i, 64)
        dst = zr.at[a, i, s, :, cols] if s else zr.at[a, i, 0, pl.ds(0, 64), cols]
        return remote(
            T.at[a, rows, cols], dst, zbs.at[k, s, i], zbr.at[k, s, i], at(0, 0, way, 0)
        )

    bc = {(k, s, w): bcopy(k, s, w) for k in range(NP) for s in range(4) for w in (1, -1)}

    def combine(k):
        a, q = k // NQ, k % NQ
        for r in range(8):
            if r:
                rc[a, q, r].wait_recv()
            else:
                rc[a, q, r].wait()
        cols = slice(q * QC, (q + 1) * QC)
        for n in range(2):
            half = slice(n * 512, (n + 1) * 512)
            T[a, half, cols] = dot(S[1 - a, :, half], ret[a, :, cols], 0, 0).astype(BF)
        for w in (1, -1):
            bc[k, 0, w].start()

    def pass_on(k, s):
        a, q = k // NQ, k % NQ
        cols = slice(q * QC, (q + 1) * QC)
        for i, w in enumerate((1, -1)):
            bc[k, s - 1, w].wait_recv()
            n = 64 if s == 1 else 128
            rows = zrow((4 - s) * w, 64 * i if s == 1 else 0, n)
            T[a, rows, cols] = (
                T[a, rows, cols].astype(F32) + zr[a, i, s - 1, 0:n, cols].astype(F32)
            ).astype(BF)
            bc[k, s, w].start()

    def finish(k):
        a, q = k // NQ, k % NQ
        cols = slice(q * QC, (q + 1) * QC)
        for w in (1, -1):
            bc[k, 3, w].wait_recv()
        rows = zrow(0)
        T[a, rows, cols] = (
            T[a, rows, cols].astype(F32)
            + zr[a, 0, 3, :, cols].astype(F32)
            + zr[a, 1, 3, :, cols].astype(F32)
        ).astype(BF)

    outs = (mixed_o, gtok_o)

    def hand_over(a):
        theirs = pl.ds(pl.multiple_of(z * 128 + (1 - c) * TOK, TOK), TOK)
        ours = pl.ds(pl.multiple_of(z * 128 + c * TOK, TOK), TOK)
        cp = remote(T.at[a, theirs, :], tw.at[a], os_.at[a], orv.at[a], at(0, 0, 0, 1))
        cp.start()
        keep = pltpu.make_async_copy(T.at[a, ours, :], outs[a].at[:, mine], ol.at[a])
        keep.start()
        return cp, keep

    def take_over(a, pair):
        cp, keep = pair
        cp.wait_recv()
        last = pltpu.make_async_copy(tw.at[a], outs[a].at[:, other], ol.at[2 + a])
        last.start()
        tail.extend((keep, last))

    pairs = {}
    for t in range(NP + 4):
        for k in range(max(0, t - 4), min(t, NP)):
            if t - k < 4:
                pass_on(k, t - k)
            else:
                finish(k)
                if k % NQ == NQ - 1:
                    pairs[k // NQ] = hand_over(k // NQ)
        if t < NP:
            combine(t)
        if t in (1, 2):
            xadd(t - 1)
        if t == NP - 2:
            xfinish(2)
        if t == NP:
            take_over(0, pairs[0])
            xfinish(0)
    take_over(1, pairs[1])
    xfinish(1)

    for cp, far in metas:
        if far:
            cp.wait_send()
    for a in range(2):
        for q in range(NQ):
            for r in range(1, 8):
                rc[a, q, r].wait_send()
    for key in bc:
        bc[key].wait_send()
    for a in range(2):
        pairs[a][0].wait_send()
    for key in xc1:
        xc1[key].wait_send()
        xc2[key].wait_send()
    for cp in tail:
        cp.wait()


def place_outputs(a, b, g, a_o, b_o, g_o, va, vb, vg, s_in, s_out):
    moves = [(g.at[m], vg.at[m], g_o.at[m]) for m in range(3)] + [(a, va, a_o), (b, vb, b_o)]
    into = [pltpu.make_async_copy(u, v, s_in.at[i]) for i, (u, v, _) in enumerate(moves)]
    out = [pltpu.make_async_copy(v, w, s_out.at[i]) for i, (_, v, w) in enumerate(moves)]
    for cp in into:
        cp.start()
    for cp, nxt in zip(into, out):
        cp.wait()
        nxt.start()
    for cp in out:
        cp.wait()


def local(tokens, expert_ids, gates, cotangent, w_gate, w_up, w_down):
    vmem = pl.BlockSpec(memory_space=pltpu.VMEM)
    hbm = pl.BlockSpec(memory_space=pl.ANY)
    dma = pltpu.SemaphoreType.DMA
    shapes = (
        jax.ShapeDtypeStruct((TOK, D), BF),
        jax.ShapeDtypeStruct((TOK, D), BF),
        jax.ShapeDtypeStruct((3, SHARE, D), BF),
    )
    results = pl.pallas_call(
        kernel,
        out_shape=shapes,
        in_specs=[vmem] * 4 + [hbm] * 3,
        out_specs=(hbm, hbm, hbm),
        scratch_shapes=[
            pltpu.VMEM((2, 16 * TOK, HALF), BF),
            pltpu.VMEM((2, 8 * BLK, 16 * TOK), BF),
            pltpu.VMEM((NZ, 16, 128), F32),
            pltpu.VMEM((2 * NZ, 16, 128), F32),
            pltpu.VMEM((8, 16 * TOK), F32),
            pltpu.VMEM((8, 16 * TOK), F32),
            pltpu.VMEM((2, 8 * BLK, HALF), BF),
            pltpu.VMEM((2, ROWS, D), BF),
            pltpu.VMEM((D, FF), BF),
            pltpu.VMEM((D, FF), BF),
            pltpu.VMEM((FF, D), BF),
            pltpu.VMEM((3, ROWS, FF), BF),
            pltpu.VMEM((2, 8 * BLK, HALF), BF),
            pltpu.VMEM((2, 2, 4, 128, HALF), BF),
            pltpu.VMEM((NX, 3, 2, SHARE, HALF), BF),
            pltpu.VMEM((2, 3, 2, SHARE // 2, HALF), BF),
            pltpu.VMEM((2, 3, 2, SHARE, HALF), BF),
            pltpu.VMEM((2, TOK, HALF), BF),
            dma((3,)), dma((2,)), dma((2,)), dma((2,)),
            dma((NZ, 2)), dma((NZ, 2)),
            dma((2 * NQ, 4, 2)), dma((2 * NQ, 4, 2)),
            dma((2 * NQ, 8)), dma((2 * NQ, 8)),
            dma((2, NQ, 8)), dma((2, NQ, 8)),
            dma((2 * NQ, 4, 2)), dma((2 * NQ, 4, 2)),
            dma((2, 2 + NQ, 2)), dma((2, 2 + NQ, 2)),
            dma((2,)), dma((2,)), dma((10,)),
        ],
        compiler_params=pltpu.CompilerParams(
            collective_id=0, has_side_effects=True, vmem_limit_bytes=60 * 2**20
        ),
        cost_estimate=pl.CostEstimate(
            flops=30_000_000_000, bytes_accessed=20_000_000, transcendentals=450_000
        ),
        name="moe",
    )(tokens, cotangent, expert_ids.T, gates.T, w_gate[0], w_up[0], w_down[0])
    mixed, grad_tokens, grads = pl.pallas_call(
        place_outputs,
        out_shape=shapes,
        in_specs=[hbm] * 3,
        out_specs=(hbm, hbm, hbm),
        scratch_shapes=[
            pltpu.VMEM((TOK, D), BF),
            pltpu.VMEM((TOK, D), BF),
            pltpu.VMEM((3, SHARE, D), BF),
            dma((5,)), dma((5,)),
        ],
        name="place_outputs",
    )(*results)
    return mixed, grad_tokens, grads.transpose(1, 0, 2)[None]


def solution(mesh):
    return jax.shard_map(
        local,
        mesh=mesh,
        in_specs=(
            P(("dp", "expert"), None),
            P(("dp", "expert"), None),
            P(("dp", "expert"), None),
            P(("dp", "expert"), None),
            P("expert", None, None),
            P("expert", None, None),
            P("expert", None, None),
        ),
        out_specs=(
            P(("dp", "expert"), None),
            P(("dp", "expert"), None),
            P("expert", "dp", None, None),
        ),
        check_vma=False,
    )
```

```python
import jax
import jax.numpy as jnp
from jax import lax
from jax.experimental import pallas as pl
from jax.experimental.pallas import tpu as pltpu
from jax.sharding import PartitionSpec as P

MESH = pl.DeviceIdType.MESH
BF = jnp.bfloat16
F32 = jnp.float32

NX, NY, NZ = 4, 4, 8
D, FF, TOK, TOP, CAP = 2048, 768, 64, 8, 9
HALF = D // 2
BLK = 16 * CAP
ROWS = NY * BLK
SHARE = FF // NX
QC = 256
NQ = HALF // QC
FULL = [(n * QC, QC) for n in range(NQ)]
OUT = [(0, a, b) for a, b in [(0, 128), (128, 128)] + FULL[1:]] + [(1, a, b) for a, b in FULL]
BACK = [(0, a, b) for a, b in FULL] + [(1, a, b) for a, b in FULL[:-1] + [(768, 128), (896, 128)]]
NT = len(OUT) - NQ
WIDE = 512
ORDER = (2, 6, 4, 3, 7, 5, 1, 0)


def dot(a, b, ca, cb):
    return lax.dot_general(a, b, (((ca,), (cb,)), ((), ())), preferred_element_type=F32)


class Both:
    def __init__(self, *copies):
        self.copies = copies

    def start(self):
        for cp in self.copies:
            cp.start()

    def wait_recv(self):
        for cp in self.copies:
            cp.wait_recv()

    def wait_send(self):
        for cp in self.copies:
            cp.wait_send()


def kernel(
    tok, cot, ids, gates, wg_h, wu_h, wd_h,
    mixed_o, gtok_o, gw_o,
    T, S, meta_s, meta_r, pos, gat, yb, xin, wg, wu, wd, act, ret, zr, zl, G, xr1, xr2, tw, ob,
    w_sem, fs, fr, tws, twr, tls, ms, mr, zs, zrv, ys, yr, rs, rr, zbs, zbr, zls, zlr, xs, xrv,
    os_, orv, ol,
):
    x = lax.axis_index("dp")
    e = lax.axis_index("expert")
    y, z, c = e // 16, lax.rem(e // 2, NZ), lax.rem(e, 2)

    def at(dx, dy, dz, dc):
        return (
            lax.rem(x + dx + NX, NX),
            (lax.rem(y + dy + NY, NY) * NZ + lax.rem(z + dz + NZ, NZ)) * 2 + lax.rem(c + dc, 2),
        )

    def remote(src, dst, ssem, rsem, where):
        return pltpu.make_async_remote_copy(
            src_ref=src, dst_ref=dst, send_sem=ssem, recv_sem=rsem,
            device_id=where, device_id_type=MESH,
        )

    w_in = [
        pltpu.make_async_copy(src, dst, w_sem.at[i])
        for i, (src, dst) in enumerate(((wg_h, wg), (wu_h, wu), (wd_h, wd)))
    ]
    for cp in w_in:
        cp.start()

    idv = ids[...]
    place = ((idv >> 1) & 7) * 8 + (idv >> 4) * 2 + (idv & 1)
    row = lax.broadcasted_iota(jnp.int32, (64, TOK), 0)
    named = jnp.zeros((64, TOK), F32)
    gated = jnp.zeros((64, TOK), F32)
    for k in range(TOP):
        hit = place[k : k + 1, :] == row
        named = named + jnp.where(hit, 1.0, 0.0)
        gated = gated + jnp.where(hit, gates[k : k + 1, :], 0.0)
    t0 = lax.broadcasted_iota(jnp.int32, (TOK, 128), 0)
    l0 = lax.broadcasted_iota(jnp.int32, (TOK, 128), 1) - TOK * c
    same = jnp.where(t0 == l0, 1.0, 0.0).astype(BF)
    upto = jnp.where(t0 <= l0, jnp.where(l0 < TOK, 1.0, 0.0), 0.0).astype(BF)
    named = named.astype(BF)
    rank = dot(named, upto, 1, 0) * dot(named, same, 1, 0)
    gate_t = dot(gated.astype(BF), same, 1, 0)
    for k in range(NZ):
        meta_s[k, 0:8, :] = rank[k * 8 : k * 8 + 8]
        meta_s[k, 8:16, :] = gate_t[k * 8 : k * 8 + 8]

    greet = [(0, 0, dz, dc) for dz in range(NZ) for dc in range(2) if dz or dc]
    greet += [(0, dy, 0, dc) for dy in range(1, NY) for dc in range(2)]
    greet += [(1, 0, 0, 0), (-1, 0, 0, 0)]
    bar = pltpu.get_barrier_semaphore()
    for g in greet:
        pl.semaphore_signal(bar, inc=1, device_id=at(*g), device_id_type=MESH)
    pl.semaphore_wait(bar, len(greet))

    def zrow(dz, lo=0, n=128):
        return pl.ds(pl.multiple_of(lax.rem(z + dz + NZ, NZ) * 128 + lo, 16), n)

    mine = pl.ds(pl.multiple_of(c * HALF, HALF), HALF)
    other = pl.ds(pl.multiple_of((1 - c) * HALF, HALF), HALF)

    my_slot = pl.ds(pl.multiple_of(z * 128 + c * TOK, TOK), TOK)

    def first(way):
        i = 0 if way == 1 else 1
        _, lo, n = OUT[0]
        return Both(*(
            remote(
                tok.at[:, pl.ds(pl.multiple_of(lax.rem(c + dc, 2) * HALF + lo, 128), n)],
                T.at[0, my_slot, pl.ds(lo, n)], fs.at[i, dc], fr.at[i, dc], at(0, 0, way, dc),
            )
            for dc in range(2)
        ))

    begin = {w: first(w) for w in (1, -1)}
    for w in (1, -1):
        begin[w].start()
    swaps, keeps = [], []
    for a, src in enumerate((tok, cot)):
        cp = remote(src.at[:, other], T.at[a, my_slot, :], tws.at[a], twr.at[a], at(0, 0, 0, 1))
        cp.start()
        swaps.append(cp)
        cp = pltpu.make_async_copy(src.at[:, mine], T.at[a, my_slot, :], tls.at[a])
        cp.start()
        keeps.append(cp)

    metas = []
    for dz in (1, 7, 2, 6, 3, 5, 4, 0):
        for dc in (0, 1):
            src = meta_s.at[lax.rem(z + dz, NZ)]
            dst = meta_r.at[z * 2 + c]
            if dz == 0 and dc == 0:
                cp = pltpu.make_async_copy(src, dst, mr.at[0, 0])
            else:
                cp = remote(src, dst, ms.at[dz, dc], mr.at[dz, dc], at(0, 0, dz, dc))
            cp.start()
            metas.append((cp, dz or dc))

    NP = len(OUT)

    def zcopy(p, s, way):
        if p == 0 and s == 0:
            return begin[way]
        a, lo, n = OUT[p]
        cols = pl.ds(lo, n)
        rows = zrow(-s * way) if s < 3 else zrow(-3 * way, 0 if way == 1 else 64, 64)
        i = 0 if way == 1 else 1
        return remote(
            T.at[a, rows, cols], T.at[a, rows, cols],
            zs.at[p, s, i], zrv.at[p, s, i], at(0, 0, way, 0),
        )

    zc = {(p, s, w): zcopy(p, s, w) for p in range(NP) for s in range(4) for w in (1, -1)}

    def zstart(p, s):
        for w in (1, -1):
            if s:
                zc[p, s - 1, w].wait_recv()
            zc[p, s, w].start()

    def target(r):
        return at(0, r // 2, 0, r % 2)

    my_rows = pl.ds(pl.multiple_of(y * BLK, 16), BLK)

    def ycopy(p, r):
        a, lo, n = OUT[p]
        src = yb.at[a, pl.ds(r * BLK, BLK), pl.ds(lo, n)]
        dst = xin.at[a, my_rows, pl.ds(pl.multiple_of(c * HALF + lo, 128), n)]
        if r == 0:
            return pltpu.make_async_copy(src, dst, yr.at[p, 0])
        return remote(src, dst, ys.at[p, r], yr.at[p, r], target(r))

    yc = {(p, r): ycopy(p, r) for p in range(NP) for r in range(8)}

    def select(p, dy):
        a, lo, n = OUT[p]
        block = slice(2 * dy * BLK, 2 * (dy + 1) * BLK)
        cols = slice(lo, lo + n)
        yb[a, block, cols] = dot(S[a, block, :], T[a, :, cols], 1, 0).astype(BF)
        yc[p, 2 * dy + 1].start()
        yc[p, 2 * dy].start()

    for a in range(2):
        swaps[a].wait_recv()
        keeps[a].wait()
    zstart(1, 0)
    zstart(0, 1)

    def places():
        for cp, far in metas:
            if far:
                cp.wait_recv()
            else:
                cp.wait()
        lane8 = lax.broadcasted_iota(jnp.int32, (8, 128), 1)
        for k in range(NZ):
            enc = meta_r[2 * k, 0:8, :] + meta_r[2 * k + 1, 0:8, :]
            base = jnp.where(lane8 < TOK, 2.0 * k * CAP - 1.0, (2.0 * k + 1.0) * CAP - 1.0)
            pos[:, k * 128 : (k + 1) * 128] = jnp.where(enc > 0.5, enc + base, -1.0)
            gat[:, k * 128 : (k + 1) * 128] = meta_r[2 * k, 8:16, :] + meta_r[2 * k + 1, 8:16, :]

    def build(r, carry):
        row16 = lax.broadcasted_iota(jnp.int32, (16, 16 * TOK), 0).astype(F32)
        j = lax.rem(y + r // 2, NY) * 2 + lax.rem(c + r, 2)
        prow = pos[pl.ds(j, 1), :]
        grow = gat[pl.ds(j, 1), :]
        for i in range(BLK // 16):
            hit = row16 + float(16 * i) == prow
            at_rows = pl.ds(pl.multiple_of(r * BLK + 16 * i, 16), 16)
            S[0, at_rows, :] = jnp.where(hit, 1.0, 0.0).astype(BF)
            S[1, at_rows, :] = jnp.where(hit, grow, 0.0).astype(BF)
        return carry

    def arrived(p):
        for r in range(8):
            if r:
                yc[p, r].wait_recv()
                yc[p, r].wait_send()
            else:
                yc[p, r].wait()

    HR = ROWS // 2

    def forward(n):
        def part(i, carry):
            rows = pl.ds(pl.multiple_of(i * HR, 16), HR)
            cols = slice(n * 256, (n + 1) * 256)
            v = xin[0, rows, :]
            g = dot(v, wg[:, cols], 1, 0)
            u = dot(v, wu[:, cols], 1, 0)
            sg = jax.nn.sigmoid(g)
            silu = g * sg
            act[0, rows, cols] = (silu * u).astype(BF)
            act[1, rows, cols] = (u * sg * (1.0 + g * (1.0 - sg))).astype(BF)
            act[2, rows, cols] = silu.astype(BF)
            return carry

        lax.fori_loop(0, 2, part, 0)

    DY = (1, 3, 2, 0)
    for t in range(2, NP + 4):
        if t >= 4:
            for w in (1, -1):
                zc[t - 4, 3, w].wait_recv()
        for i in range(4):
            k = t - 3 + i
            if t >= 4:
                select(t - 4, DY[i])
            if 0 <= k < NP:
                zstart(k, t - k)
        if t == 2:
            places()
        if t == 3:
            lax.fori_loop(0, 8, build, 0)
        if t == NT + 4:
            for p in range(NT):
                arrived(p)
            for cp in w_in:
                cp.wait()
        if NT + 4 <= t < NT + 4 + FF // 256:
            forward(t - NT - 4)

    def give_back(a, q, h, rows):
        for k in range(NY):
            r = lax.rem(k - y + NY, NY) * 2 + lax.rem(h - c + 2, 2)
            yb[a, pl.ds(pl.multiple_of(r * BLK, 16), BLK), q * WIDE : (q + 1) * WIDE] = (
                rows[k * BLK : (k + 1) * BLK].astype(BF)
            )

    def rcopy(k, r):
        a, lo, n = BACK[k]
        cols = pl.ds(lo, n)
        there = (NY - r // 2) % NY * 2 + r % 2
        src = yb.at[a, pl.ds(r * BLK, BLK), cols]
        dst = ret.at[a, pl.ds(there * BLK, BLK), cols]
        if r == 0:
            return pltpu.make_async_copy(src, dst, rr.at[k, 0])
        return remote(src, dst, rs.at[k, r], rr.at[k, r], target(r))

    NB = len(BACK)
    rc = {(k, r): rcopy(k, r) for k in range(NB) for r in range(8)}

    def send_back(a, q):
        for k in range(NB):
            if BACK[k][0] == a and BACK[k][1] // WIDE == q:
                for r in ORDER:
                    rc[k, r].start()

    for q in range(HALF // WIDE):
        for h in range(2):
            n = h * HALF + q * WIDE
            give_back(0, q, h, dot(act[0], wd[:, n : n + WIDE], 1, 0))
        send_back(0, q)

    def xshare(dx):
        return lax.rem(x + dx + NX, NX)

    SH2 = SHARE // 2

    def piece(n):
        if n < 2:
            return n, slice(0, HALF)
        return 2, slice((n - 2) * QC, (n - 1) * QC)

    PIECES = 2 + NQ

    def xcopy1(n, way):
        i = 0 if way == 1 else 1
        m, cols = piece(n)
        return remote(
            G.at[xshare(2), m, :, pl.ds(i * SH2, SH2), cols], xr1.at[i, m, :, :, cols],
            xs.at[0, n, i], xrv.at[0, n, i], at(way, 0, 0, 0),
        )

    def xcopy2(n, way):
        i = 0 if way == 1 else 1
        m, cols = piece(n)
        return remote(
            G.at[xshare(way), m, :, :, cols], xr2.at[i, m, :, :, cols],
            xs.at[1, n, i], xrv.at[1, n, i], at(way, 0, 0, 0),
        )

    xc1 = {(n, w): xcopy1(n, w) for n in range(PIECES) for w in (1, -1)}
    xc2 = {(n, w): xcopy2(n, w) for n in range(PIECES) for w in (1, -1)}

    def product(m, b, k, h, cols, at_cols):
        for hf in range(2):
            v = dot(act[k, :, hf * 384 : (hf + 1) * 384], xin[b, :, cols], 0, 0).astype(BF)
            G[2 * hf, m, h, :, at_cols] = v[:SHARE]
            G[2 * hf + 1, m, h, :, at_cols] = v[SHARE:]

    def weights(m, b, k):
        def part(i, carry):
            here = pl.ds(pl.multiple_of(i * WIDE, WIDE), WIDE)
            for h in range(2):
                cols = pl.ds(pl.multiple_of(h * HALF + i * WIDE, WIDE), WIDE)
                product(m, b, k, h, cols, here)
            return carry

        lax.fori_loop(0, HALF // WIDE, part, 0)
        for w in (1, -1):
            xc1[m, w].start()

    def xadd(n):
        m, cols = piece(n)
        for i, w in enumerate((1, -1)):
            xc1[n, w].wait_recv()
            rows = pl.ds(i * SH2, SH2)
            d = xshare(w)
            for h in range(2):
                G[d, m, h, rows, cols] = (
                    G[d, m, h, rows, cols].astype(F32) + xr1[i, m, h, :, cols].astype(F32)
                ).astype(BF)
            xc2[n, w].start()

    def xfinish(m):
        for n in range(PIECES):
            if piece(n)[0] == m:
                for w in (1, -1):
                    xc2[n, w].wait_recv()
        own = xshare(0)
        for h in range(2):
            G[own, m, h] = (
                G[own, m, h].astype(F32) + xr2[0, m, h].astype(F32) + xr2[1, m, h].astype(F32)
            ).astype(BF)
            cp = pltpu.make_async_copy(
                G.at[own, m, h], gw_o.at[m, :, pl.ds(h * HALF, HALF)], ol.at[4 + 2 * m + h]
            )
            cp.start()
            tail.append(cp)

    tail = []
    for i in range(NQ):
        arrived(NT + i)
        for h in range(2):
            n = h * HALF + i * QC
            product(2, 1, 0, h, slice(n, n + QC), slice(i * QC, (i + 1) * QC))
        for w in (1, -1):
            xc1[2 + i, w].start()
        if i:
            xadd(1 + i)

    def backward(i, carry):
        cols = pl.ds(pl.multiple_of(i * 256, 256), 256)
        g = dot(xin[1], wd[cols, :], 1, 1)
        act[1, :, cols] = (g * act[1, :, cols].astype(F32)).astype(BF)
        act[2, :, cols] = (g * act[2, :, cols].astype(F32)).astype(BF)
        return carry

    lax.fori_loop(0, FF // 256, backward, 0)
    weights(0, 0, 1)
    weights(1, 0, 2)
    xadd(1 + NQ)
    for q in range(HALF // WIDE):
        for h in range(2):
            n = h * HALF + q * WIDE
            give_back(
                1, q, h,
                dot(act[1], wg[n : n + WIDE, :], 1, 1) + dot(act[2], wu[n : n + WIDE, :], 1, 1),
            )
        send_back(1, q)

    for a in range(2):
        swaps[a].wait_send()
    for key in zc:
        zc[key].wait_send()

    own_rows = {0: my_slot, 1: pl.ds(pl.multiple_of(z * 128 + (1 - c) * TOK, TOK), TOK)}

    def bcopy(k, s, way):
        a, lo, n = BACK[k]
        i = 0 if way == 1 else 1
        cols = pl.ds(lo, n)
        if s == 3:
            return Both(*(
                remote(
                    T.at[a, zrow(way, lax.rem(c + dc, 2) * TOK, TOK), cols],
                    zl.at[a, i, c, :, cols], zls.at[k, i, dc], zlr.at[k, i, dc],
                    at(0, 0, way, dc),
                )
                for dc in range(2)
            ))
        rows = zrow((4 - s) * way) if s else zrow(4, 64 * i, 64)
        dst = zr.at[a, i, s, :, cols] if s else zr.at[a, i, 0, pl.ds(0, 64), cols]
        return remote(
            T.at[a, rows, cols], dst, zbs.at[k, s, i], zbr.at[k, s, i], at(0, 0, way, 0)
        )

    def tcopy(k):
        a, lo, n = BACK[k]
        cols = pl.ds(lo, n)
        return remote(
            T.at[a, own_rows[1], cols], tw.at[a, :, cols], os_.at[k], orv.at[k], at(0, 0, 0, 1)
        )

    bc = {(k, s, w): bcopy(k, s, w) for k in range(NB) for s in range(4) for w in (1, -1)}
    tc = {(k,): tcopy(k) for k in range(NB)}

    def combine(k):
        a, lo, n = BACK[k]
        for r in range(8):
            if r:
                rc[k, r].wait_recv()
            else:
                rc[k, r].wait()
        cols = slice(lo, lo + n)
        for j in range(2):
            half = slice(j * 512, (j + 1) * 512)
            T[a, half, cols] = dot(S[1 - a, :, half], ret[a, :, cols], 0, 0).astype(BF)
        for w in (1, -1):
            bc[k, 0, w].start()
        tc[k,].start()

    def pass_on(k, s):
        a, lo, n = BACK[k]
        cols = slice(lo, lo + n)
        for i, w in enumerate((1, -1)):
            bc[k, s - 1, w].wait_recv()
            m = 64 if s == 1 else 128
            rows = zrow((4 - s) * w, 64 * i if s == 1 else 0, m)
            T[a, rows, cols] = (
                T[a, rows, cols].astype(F32) + zr[a, i, s - 1, 0:m, cols].astype(F32)
            ).astype(BF)
            bc[k, s, w].start()

    def finish(k):
        a, lo, n = BACK[k]
        cols = slice(lo, lo + n)
        for w in (1, -1):
            bc[k, 3, w].wait_recv()
        tc[k,].wait_recv()
        for h, mid in ((c, T[a, own_rows[0], cols]), (1 - c, tw[a, :, cols])):
            ob[a, h, :, cols] = (
                mid.astype(F32)
                + zl[a, 0, h, :, cols].astype(F32)
                + zl[a, 1, h, :, cols].astype(F32)
            ).astype(BF)

    outs = (mixed_o, gtok_o)

    def deliver(a):
        for h in range(2):
            cp = pltpu.make_async_copy(
                ob.at[a, h], outs[a].at[:, pl.ds(h * HALF, HALF)], ol.at[2 * a + h]
            )
            cp.start()
            tail.append(cp)

    for t in range(NB + 4):
        for k in range(max(0, t - 4), min(t, NB)):
            if t - k < 4:
                pass_on(k, t - k)
            else:
                finish(k)
                if k == NQ - 1:
                    deliver(0)
        if t < NB:
            combine(t)
        if t in (1, 2):
            xadd(t - 1)
        if t == NB - 2:
            xfinish(2)
        if t == NB:
            xfinish(0)
    deliver(1)
    xfinish(1)

    for cp, far in metas:
        if far:
            cp.wait_send()
    for key in rc:
        if key[1]:
            rc[key].wait_send()
    for key in tc:
        tc[key].wait_send()
    for key in bc:
        bc[key].wait_send()
    for key in xc1:
        xc1[key].wait_send()
        xc2[key].wait_send()
    for cp in tail:
        cp.wait()


def place_outputs(a, b, g, a_o, b_o, g_o, va, vb, vg, s_in, s_out):
    moves = [(g.at[m], vg.at[m], g_o.at[m]) for m in range(3)] + [(a, va, a_o), (b, vb, b_o)]
    into = [pltpu.make_async_copy(u, v, s_in.at[i]) for i, (u, v, _) in enumerate(moves)]
    out = [pltpu.make_async_copy(v, w, s_out.at[i]) for i, (_, v, w) in enumerate(moves)]
    for cp in into:
        cp.start()
    for cp, nxt in zip(into, out):
        cp.wait()
        nxt.start()
    for cp in out:
        cp.wait()


def local(tokens, expert_ids, gates, cotangent, w_gate, w_up, w_down):
    vmem = pl.BlockSpec(memory_space=pltpu.VMEM)
    hbm = pl.BlockSpec(memory_space=pl.ANY)
    dma = pltpu.SemaphoreType.DMA
    shapes = (
        jax.ShapeDtypeStruct((TOK, D), BF),
        jax.ShapeDtypeStruct((TOK, D), BF),
        jax.ShapeDtypeStruct((3, SHARE, D), BF),
    )
    results = pl.pallas_call(
        kernel,
        out_shape=shapes,
        in_specs=[vmem] * 4 + [hbm] * 3,
        out_specs=(hbm, hbm, hbm),
        scratch_shapes=[
            pltpu.VMEM((2, 16 * TOK, HALF), BF),
            pltpu.VMEM((2, 8 * BLK, 16 * TOK), BF),
            pltpu.VMEM((NZ, 16, 128), F32),
            pltpu.VMEM((2 * NZ, 16, 128), F32),
            pltpu.VMEM((8, 16 * TOK), F32),
            pltpu.VMEM((8, 16 * TOK), F32),
            pltpu.VMEM((2, 8 * BLK, HALF), BF),
            pltpu.VMEM((2, ROWS, D), BF),
            pltpu.VMEM((D, FF), BF),
            pltpu.VMEM((D, FF), BF),
            pltpu.VMEM((FF, D), BF),
            pltpu.VMEM((3, ROWS, FF), BF),
            pltpu.VMEM((2, 8 * BLK, HALF), BF),
            pltpu.VMEM((2, 2, 3, 128, HALF), BF),
            pltpu.VMEM((2, 2, 2, TOK, HALF), BF),
            pltpu.VMEM((NX, 3, 2, SHARE, HALF), BF),
            pltpu.VMEM((2, 3, 2, SHARE // 2, HALF), BF),
            pltpu.VMEM((2, 3, 2, SHARE, HALF), BF),
            pltpu.VMEM((2, TOK, HALF), BF),
            pltpu.VMEM((2, 2, TOK, HALF), BF),
            dma((3,)), dma((2, 2)), dma((2, 2)), dma((2,)), dma((2,)), dma((2,)),
            dma((NZ, 2)), dma((NZ, 2)),
            dma((len(OUT), 4, 2)), dma((len(OUT), 4, 2)),
            dma((len(OUT), 8)), dma((len(OUT), 8)),
            dma((len(BACK), 8)), dma((len(BACK), 8)),
            dma((len(BACK), 3, 2)), dma((len(BACK), 3, 2)),
            dma((len(BACK), 2, 2)), dma((len(BACK), 2, 2)),
            dma((2, 2 + NQ, 2)), dma((2, 2 + NQ, 2)),
            dma((len(BACK),)), dma((len(BACK),)), dma((10,)),
        ],
        compiler_params=pltpu.CompilerParams(
            collective_id=0, has_side_effects=True, vmem_limit_bytes=60 * 2**20
        ),
        cost_estimate=pl.CostEstimate(
            flops=30_000_000_000, bytes_accessed=20_000_000, transcendentals=450_000
        ),
        name="moe",
    )(tokens, cotangent, expert_ids.T, gates.T, w_gate[0], w_up[0], w_down[0])
    mixed, grad_tokens, grads = pl.pallas_call(
        place_outputs,
        out_shape=shapes,
        in_specs=[hbm] * 3,
        out_specs=(hbm, hbm, hbm),
        scratch_shapes=[
            pltpu.VMEM((TOK, D), BF),
            pltpu.VMEM((TOK, D), BF),
            pltpu.VMEM((3, SHARE, D), BF),
            dma((5,)), dma((5,)),
        ],
        name="place_outputs",
    )(*results)
    return mixed, grad_tokens, grads.transpose(1, 0, 2)[None]


def solution(mesh):
    return jax.shard_map(
        local,
        mesh=mesh,
        in_specs=(
            P(("dp", "expert"), None),
            P(("dp", "expert"), None),
            P(("dp", "expert"), None),
            P(("dp", "expert"), None),
            P("expert", None, None),
            P("expert", None, None),
            P("expert", None, None),
        ),
        out_specs=(
            P(("dp", "expert"), None),
            P(("dp", "expert"), None),
            P("expert", "dp", None, None),
        ),
        check_vma=False,
    )
```

```python
import jax
import jax.numpy as jnp
from jax import lax
from jax.experimental import pallas as pl
from jax.experimental.pallas import tpu as pltpu
from jax.sharding import PartitionSpec as P

MESH = pl.DeviceIdType.MESH
BF = jnp.bfloat16
F32 = jnp.float32

NX, NY, NZ = 4, 4, 8
D, FF, TOK, TOP, CAP = 2048, 768, 64, 8, 9
HALF = D // 2
BLK = 16 * CAP
ROWS = NY * BLK
SHARE = FF // NX
QC = 256
NQ = HALF // QC
FULL = [(n * QC, QC) for n in range(NQ)]
OUT = [(0, a, b) for a, b in [(0, 128), (128, 128)] + FULL[1:]] + [(1, a, b) for a, b in FULL]
BACK = [(0, a, b) for a, b in FULL] + [(1, a, b) for a, b in FULL[:-1] + [(768, 128), (896, 128)]]
NT = len(OUT) - NQ
WIDE = 512
ORDER = (2, 6, 4, 3, 7, 5, 1, 0)


def dot(a, b, ca, cb):
    return lax.dot_general(a, b, (((ca,), (cb,)), ((), ())), preferred_element_type=F32)


class Both:
    def __init__(self, *copies):
        self.copies = copies

    def start(self):
        for cp in self.copies:
            cp.start()

    def wait_recv(self):
        for cp in self.copies:
            cp.wait_recv()

    def wait_send(self):
        for cp in self.copies:
            cp.wait_send()


def kernel(
    tok, cot, ids, gates, wg_h, wu_h, wd_h,
    mixed_o, gtok_o, gw_o,
    T, S, meta_s, meta_r, pos, gat, yb, xin, wg, wu, wd, act, ret, zr, zl, G, xr1, xr2, tw, ob,
    w_sem, fs, fr, tws, twr, tls, ms, mr, zs, zrv, ys, yr, rs, rr, zbs, zbr, zls, zlr, xs, xrv,
    os_, orv, ol,
):
    x = lax.axis_index("dp")
    e = lax.axis_index("expert")
    y, z, c = e // 16, lax.rem(e // 2, NZ), lax.rem(e, 2)

    def at(dx, dy, dz, dc):
        return (
            lax.rem(x + dx + NX, NX),
            (lax.rem(y + dy + NY, NY) * NZ + lax.rem(z + dz + NZ, NZ)) * 2 + lax.rem(c + dc, 2),
        )

    def remote(src, dst, ssem, rsem, where):
        return pltpu.make_async_remote_copy(
            src_ref=src, dst_ref=dst, send_sem=ssem, recv_sem=rsem,
            device_id=where, device_id_type=MESH,
        )

    w_in = [
        pltpu.make_async_copy(src, dst, w_sem.at[i])
        for i, (src, dst) in enumerate(((wg_h, wg), (wu_h, wu), (wd_h, wd)))
    ]
    for cp in w_in:
        cp.start()

    idv = ids[...]
    place = ((idv >> 1) & 7) * 8 + (idv >> 4) * 2 + (idv & 1)
    row = lax.broadcasted_iota(jnp.int32, (64, TOK), 0)
    named = jnp.zeros((64, TOK), F32)
    gated = jnp.zeros((64, TOK), F32)
    for k in range(TOP):
        hit = place[k : k + 1, :] == row
        named = named + jnp.where(hit, 1.0, 0.0)
        gated = gated + jnp.where(hit, gates[k : k + 1, :], 0.0)
    t0 = lax.broadcasted_iota(jnp.int32, (TOK, 128), 0)
    l0 = lax.broadcasted_iota(jnp.int32, (TOK, 128), 1) - TOK * c
    same = jnp.where(t0 == l0, 1.0, 0.0).astype(BF)
    upto = jnp.where(t0 <= l0, jnp.where(l0 < TOK, 1.0, 0.0), 0.0).astype(BF)
    named = named.astype(BF)
    rank = dot(named, upto, 1, 0) * dot(named, same, 1, 0)
    gate_t = dot(gated.astype(BF), same, 1, 0)
    for k in range(NZ):
        meta_s[k, 0:8, :] = rank[k * 8 : k * 8 + 8]
        meta_s[k, 8:16, :] = gate_t[k * 8 : k * 8 + 8]

    greet = [(0, 0, dz, dc) for dz in range(NZ) for dc in range(2) if dz or dc]
    greet += [(0, dy, 0, dc) for dy in range(1, NY) for dc in range(2)]
    greet += [(1, 0, 0, 0), (-1, 0, 0, 0)]
    bar = pltpu.get_barrier_semaphore()
    for g in greet:
        pl.semaphore_signal(bar, inc=1, device_id=at(*g), device_id_type=MESH)
    pl.semaphore_wait(bar, len(greet))

    def zrow(dz, lo=0, n=128):
        return pl.ds(pl.multiple_of(lax.rem(z + dz + NZ, NZ) * 128 + lo, 16), n)

    mine = pl.ds(pl.multiple_of(c * HALF, HALF), HALF)
    other = pl.ds(pl.multiple_of((1 - c) * HALF, HALF), HALF)

    my_slot = pl.ds(pl.multiple_of(z * 128 + c * TOK, TOK), TOK)

    def first(way):
        i = 0 if way == 1 else 1
        _, lo, n = OUT[0]
        return Both(*(
            remote(
                tok.at[:, pl.ds(pl.multiple_of(lax.rem(c + dc, 2) * HALF + lo, 128), n)],
                T.at[0, my_slot, pl.ds(lo, n)], fs.at[i, dc], fr.at[i, dc], at(0, 0, way, dc),
            )
            for dc in range(2)
        ))

    begin = {w: first(w) for w in (1, -1)}
    for w in (1, -1):
        begin[w].start()
    swaps, keeps = [], []
    for a, src in enumerate((tok, cot)):
        cp = remote(src.at[:, other], T.at[a, my_slot, :], tws.at[a], twr.at[a], at(0, 0, 0, 1))
        cp.start()
        swaps.append(cp)
        cp = pltpu.make_async_copy(src.at[:, mine], T.at[a, my_slot, :], tls.at[a])
        cp.start()
        keeps.append(cp)

    metas = []
    for dz in (1, 7, 2, 6, 3, 5, 4, 0):
        for dc in (0, 1):
            src = meta_s.at[lax.rem(z + dz, NZ)]
            dst = meta_r.at[z * 2 + c]
            if dz == 0 and dc == 0:
                cp = pltpu.make_async_copy(src, dst, mr.at[0, 0])
            else:
                cp = remote(src, dst, ms.at[dz, dc], mr.at[dz, dc], at(0, 0, dz, dc))
            cp.start()
            metas.append((cp, dz or dc))

    NP = len(OUT)

    def zcopy(p, s, way):
        if p == 0 and s == 0:
            return begin[way]
        a, lo, n = OUT[p]
        cols = pl.ds(lo, n)
        rows = zrow(-s * way) if s < 3 else zrow(-3 * way, 0 if way == 1 else 64, 64)
        i = 0 if way == 1 else 1
        return remote(
            T.at[a, rows, cols], T.at[a, rows, cols],
            zs.at[p, s, i], zrv.at[p, s, i], at(0, 0, way, 0),
        )

    zc = {(p, s, w): zcopy(p, s, w) for p in range(NP) for s in range(4) for w in (1, -1)}

    def zstart(p, s):
        for w in (1, -1):
            if s:
                zc[p, s - 1, w].wait_recv()
            zc[p, s, w].start()

    def target(r):
        return at(0, r // 2, 0, r % 2)

    my_rows = pl.ds(pl.multiple_of(y * BLK, 16), BLK)

    def ycopy(p, r):
        a, lo, n = OUT[p]
        src = yb.at[a, pl.ds(r * BLK, BLK), pl.ds(lo, n)]
        dst = xin.at[a, my_rows, pl.ds(pl.multiple_of(c * HALF + lo, 128), n)]
        if r == 0:
            return pltpu.make_async_copy(src, dst, yr.at[p, 0])
        return remote(src, dst, ys.at[p, r], yr.at[p, r], target(r))

    yc = {(p, r): ycopy(p, r) for p in range(NP) for r in range(8)}

    def select(p, dy):
        a, lo, n = OUT[p]
        block = slice(2 * dy * BLK, 2 * (dy + 1) * BLK)
        cols = slice(lo, lo + n)
        yb[a, block, cols] = dot(S[a, block, :], T[a, :, cols], 1, 0).astype(BF)
        yc[p, 2 * dy + 1].start()
        yc[p, 2 * dy].start()

    for a in range(2):
        swaps[a].wait_recv()
        keeps[a].wait()
    zstart(1, 0)
    zstart(0, 1)

    def places():
        for cp, far in metas:
            if far:
                cp.wait_recv()
            else:
                cp.wait()
        lane8 = lax.broadcasted_iota(jnp.int32, (8, 128), 1)
        for k in range(NZ):
            enc = meta_r[2 * k, 0:8, :] + meta_r[2 * k + 1, 0:8, :]
            base = jnp.where(lane8 < TOK, 2.0 * k * CAP - 1.0, (2.0 * k + 1.0) * CAP - 1.0)
            pos[:, k * 128 : (k + 1) * 128] = jnp.where(enc > 0.5, enc + base, -1.0)
            gat[:, k * 128 : (k + 1) * 128] = meta_r[2 * k, 8:16, :] + meta_r[2 * k + 1, 8:16, :]

    def build(r, carry):
        row16 = lax.broadcasted_iota(jnp.int32, (16, 16 * TOK), 0).astype(F32)
        j = lax.rem(y + r // 2, NY) * 2 + lax.rem(c + r, 2)
        prow = pos[pl.ds(j, 1), :]
        grow = gat[pl.ds(j, 1), :]
        for i in range(BLK // 16):
            hit = row16 + float(16 * i) == prow
            at_rows = pl.ds(pl.multiple_of(r * BLK + 16 * i, 16), 16)
            S[0, at_rows, :] = jnp.where(hit, 1.0, 0.0).astype(BF)
            S[1, at_rows, :] = jnp.where(hit, grow, 0.0).astype(BF)
        return carry

    def arrived(p):
        for r in range(8):
            if r:
                yc[p, r].wait_recv()
                yc[p, r].wait_send()
            else:
                yc[p, r].wait()

    HR = ROWS // 2

    def forward(n):
        def part(i, carry):
            rows = pl.ds(pl.multiple_of(i * HR, 16), HR)
            cols = slice(n * 256, (n + 1) * 256)
            v = xin[0, rows, :]
            g = dot(v, wg[:, cols], 1, 0)
            u = dot(v, wu[:, cols], 1, 0)
            sg = jax.nn.sigmoid(g)
            silu = g * sg
            act[0, rows, cols] = (silu * u).astype(BF)
            act[1, rows, cols] = (u * sg * (1.0 + g * (1.0 - sg))).astype(BF)
            act[2, rows, cols] = silu.astype(BF)
            return carry

        lax.fori_loop(0, 2, part, 0)

    DY = (1, 3, 2, 0)
    for t in range(2, NP + 4):
        if t >= 4:
            for w in (1, -1):
                zc[t - 4, 3, w].wait_recv()
        for i in range(4):
            k = t - 3 + i
            if t >= 4:
                select(t - 4, DY[i])
            if 0 <= k < NP:
                zstart(k, t - k)
        if t == 2:
            places()
        if t == 3:
            lax.fori_loop(0, 8, build, 0)

    for p in range(NT):
        arrived(p)
    for cp in w_in:
        cp.wait()
    for n in range(FF // 256):
        forward(n)

    def give_back(a, q, h, rows):
        for k in range(NY):
            r = lax.rem(k - y + NY, NY) * 2 + lax.rem(h - c + 2, 2)
            yb[a, pl.ds(pl.multiple_of(r * BLK, 16), BLK), q * WIDE : (q + 1) * WIDE] = (
                rows[k * BLK : (k + 1) * BLK].astype(BF)
            )

    def rcopy(k, r):
        a, lo, n = BACK[k]
        cols = pl.ds(lo, n)
        there = (NY - r // 2) % NY * 2 + r % 2
        src = yb.at[a, pl.ds(r * BLK, BLK), cols]
        dst = ret.at[a, pl.ds(there * BLK, BLK), cols]
        if r == 0:
            return pltpu.make_async_copy(src, dst, rr.at[k, 0])
        return remote(src, dst, rs.at[k, r], rr.at[k, r], target(r))

    NB = len(BACK)
    rc = {(k, r): rcopy(k, r) for k in range(NB) for r in range(8)}

    def send_back(a, q):
        for k in range(NB):
            if BACK[k][0] == a and BACK[k][1] // WIDE == q:
                for r in ORDER:
                    rc[k, r].start()

    def results(q):
        for h in range(2):
            n = h * HALF + q * WIDE
            give_back(0, q, h, dot(act[0], wd[:, n : n + WIDE], 1, 0))
        send_back(0, q)

    def xshare(dx):
        return lax.rem(x + dx + NX, NX)

    SH2 = SHARE // 2

    def piece(n):
        if n < 2:
            return n, slice(0, HALF)
        return 2, slice((n - 2) * QC, (n - 1) * QC)

    PIECES = 2 + NQ

    def xcopy1(n, way):
        i = 0 if way == 1 else 1
        m, cols = piece(n)
        return remote(
            G.at[xshare(2), m, :, pl.ds(i * SH2, SH2), cols], xr1.at[i, m, :, :, cols],
            xs.at[0, n, i], xrv.at[0, n, i], at(way, 0, 0, 0),
        )

    def xcopy2(n, way):
        i = 0 if way == 1 else 1
        m, cols = piece(n)
        return remote(
            G.at[xshare(way), m, :, :, cols], xr2.at[i, m, :, :, cols],
            xs.at[1, n, i], xrv.at[1, n, i], at(way, 0, 0, 0),
        )

    xc1 = {(n, w): xcopy1(n, w) for n in range(PIECES) for w in (1, -1)}
    xc2 = {(n, w): xcopy2(n, w) for n in range(PIECES) for w in (1, -1)}

    def product(m, b, k, h, cols, at_cols):
        for hf in range(2):
            v = dot(act[k, :, hf * 384 : (hf + 1) * 384], xin[b, :, cols], 0, 0).astype(BF)
            G[2 * hf, m, h, :, at_cols] = v[:SHARE]
            G[2 * hf + 1, m, h, :, at_cols] = v[SHARE:]

    def weights(m, b, k):
        def part(i, carry):
            here = pl.ds(pl.multiple_of(i * WIDE, WIDE), WIDE)
            for h in range(2):
                cols = pl.ds(pl.multiple_of(h * HALF + i * WIDE, WIDE), WIDE)
                product(m, b, k, h, cols, here)
            return carry

        lax.fori_loop(0, HALF // WIDE, part, 0)
        for w in (1, -1):
            xc1[m, w].start()

    def xadd(n):
        m, cols = piece(n)
        for i, w in enumerate((1, -1)):
            xc1[n, w].wait_recv()
            rows = pl.ds(i * SH2, SH2)
            d = xshare(w)
            for h in range(2):
                G[d, m, h, rows, cols] = (
                    G[d, m, h, rows, cols].astype(F32) + xr1[i, m, h, :, cols].astype(F32)
                ).astype(BF)
            xc2[n, w].start()

    def xfinish(m):
        for n in range(PIECES):
            if piece(n)[0] == m:
                for w in (1, -1):
                    xc2[n, w].wait_recv()
        own = xshare(0)
        for h in range(2):
            G[own, m, h] = (
                G[own, m, h].astype(F32) + xr2[0, m, h].astype(F32) + xr2[1, m, h].astype(F32)
            ).astype(BF)
            cp = pltpu.make_async_copy(
                G.at[own, m, h], gw_o.at[m, :, pl.ds(h * HALF, HALF)], ol.at[4 + 2 * m + h]
            )
            cp.start()
            tail.append(cp)

    tail = []
    for i in range(NQ):
        arrived(NT + i)
        for h in range(2):
            n = h * HALF + i * QC
            product(2, 1, 0, h, slice(n, n + QC), slice(i * QC, (i + 1) * QC))
        for w in (1, -1):
            xc1[2 + i, w].start()
        if i:
            xadd(1 + i)
        if i < HALF // WIDE:
            results(i)

    def backward(i, carry):
        cols = pl.ds(pl.multiple_of(i * 256, 256), 256)
        g = dot(xin[1], wd[cols, :], 1, 1)
        act[1, :, cols] = (g * act[1, :, cols].astype(F32)).astype(BF)
        act[2, :, cols] = (g * act[2, :, cols].astype(F32)).astype(BF)
        return carry

    for a in range(2):
        swaps[a].wait_send()
    for key in zc:
        zc[key].wait_send()

    own_rows = {0: my_slot, 1: pl.ds(pl.multiple_of(z * 128 + (1 - c) * TOK, TOK), TOK)}

    def bcopy(k, s, way):
        a, lo, n = BACK[k]
        i = 0 if way == 1 else 1
        cols = pl.ds(lo, n)
        if s == 3:
            return Both(*(
                remote(
                    T.at[a, zrow(way, lax.rem(c + dc, 2) * TOK, TOK), cols],
                    zl.at[a, i, c, :, cols], zls.at[k, i, dc], zlr.at[k, i, dc],
                    at(0, 0, way, dc),
                )
                for dc in range(2)
            ))
        rows = zrow((4 - s) * way) if s else zrow(4, 64 * i, 64)
        dst = zr.at[a, i, s, :, cols] if s else zr.at[a, i, 0, pl.ds(0, 64), cols]
        return remote(
            T.at[a, rows, cols], dst, zbs.at[k, s, i], zbr.at[k, s, i], at(0, 0, way, 0)
        )

    def tcopy(k):
        a, lo, n = BACK[k]
        cols = pl.ds(lo, n)
        return remote(
            T.at[a, own_rows[1], cols], tw.at[a, :, cols], os_.at[k], orv.at[k], at(0, 0, 0, 1)
        )

    bc = {(k, s, w): bcopy(k, s, w) for k in range(NB) for s in range(4) for w in (1, -1)}
    tc = {(k,): tcopy(k) for k in range(NB)}

    def combine(k):
        a, lo, n = BACK[k]
        for r in range(8):
            if r:
                rc[k, r].wait_recv()
            else:
                rc[k, r].wait()
        cols = slice(lo, lo + n)
        for j in range(2):
            half = slice(j * 512, (j + 1) * 512)
            T[a, half, cols] = dot(S[1 - a, :, half], ret[a, :, cols], 0, 0).astype(BF)
        for w in (1, -1):
            bc[k, 0, w].start()
        tc[k,].start()

    def pass_on(k, s):
        a, lo, n = BACK[k]
        cols = slice(lo, lo + n)
        for i, w in enumerate((1, -1)):
            bc[k, s - 1, w].wait_recv()
            m = 64 if s == 1 else 128
            rows = zrow((4 - s) * w, 64 * i if s == 1 else 0, m)
            T[a, rows, cols] = (
                T[a, rows, cols].astype(F32) + zr[a, i, s - 1, 0:m, cols].astype(F32)
            ).astype(BF)
            bc[k, s, w].start()

    def finish(k):
        a, lo, n = BACK[k]
        cols = slice(lo, lo + n)
        for w in (1, -1):
            bc[k, 3, w].wait_recv()
        tc[k,].wait_recv()
        for h, mid in ((c, T[a, own_rows[0], cols]), (1 - c, tw[a, :, cols])):
            ob[a, h, :, cols] = (
                mid.astype(F32)
                + zl[a, 0, h, :, cols].astype(F32)
                + zl[a, 1, h, :, cols].astype(F32)
            ).astype(BF)

    outs = (mixed_o, gtok_o)

    def deliver(a):
        for h in range(2):
            cp = pltpu.make_async_copy(
                ob.at[a, h], outs[a].at[:, pl.ds(h * HALF, HALF)], ol.at[2 * a + h]
            )
            cp.start()
            tail.append(cp)

    def slot_grads(q):
        for h in range(2):
            n = h * HALF + q * WIDE
            give_back(
                1, q, h,
                dot(act[1], wg[n : n + WIDE, :], 1, 1) + dot(act[2], wu[n : n + WIDE, :], 1, 1),
            )
        send_back(1, q)

    lax.fori_loop(0, FF // 256, backward, 0)
    xadd(1 + NQ)
    weights(0, 0, 1)
    between = {
        0: lambda: weights(1, 0, 2),
        1: lambda: slot_grads(0),
        2: lambda: slot_grads(1),
        3: lambda: xadd(0),
        4: lambda: xadd(1),
        NB - 2: lambda: xfinish(2),
        NB + 2: lambda: xfinish(0),
    }
    for t in range(NB + 4):
        for k in range(max(0, t - 4), min(t, NB)):
            if t - k < 4:
                pass_on(k, t - k)
            else:
                finish(k)
                if k == NQ - 1:
                    deliver(0)
        if t < NB:
            combine(t)
        if t in between:
            between[t]()
    deliver(1)
    xfinish(1)

    for cp, far in metas:
        if far:
            cp.wait_send()
    for key in rc:
        if key[1]:
            rc[key].wait_send()
    for key in tc:
        tc[key].wait_send()
    for key in bc:
        bc[key].wait_send()
    for key in xc1:
        xc1[key].wait_send()
        xc2[key].wait_send()
    for cp in tail:
        cp.wait()


def place_outputs(a, b, g, a_o, b_o, g_o, va, vb, vg, s_in, s_out):
    moves = [(g.at[m], vg.at[m], g_o.at[m]) for m in range(3)] + [(a, va, a_o), (b, vb, b_o)]
    into = [pltpu.make_async_copy(u, v, s_in.at[i]) for i, (u, v, _) in enumerate(moves)]
    out = [pltpu.make_async_copy(v, w, s_out.at[i]) for i, (_, v, w) in enumerate(moves)]
    for cp in into:
        cp.start()
    for cp, nxt in zip(into, out):
        cp.wait()
        nxt.start()
    for cp in out:
        cp.wait()


def local(tokens, expert_ids, gates, cotangent, w_gate, w_up, w_down):
    vmem = pl.BlockSpec(memory_space=pltpu.VMEM)
    hbm = pl.BlockSpec(memory_space=pl.ANY)
    dma = pltpu.SemaphoreType.DMA
    shapes = (
        jax.ShapeDtypeStruct((TOK, D), BF),
        jax.ShapeDtypeStruct((TOK, D), BF),
        jax.ShapeDtypeStruct((3, SHARE, D), BF),
    )
    results = pl.pallas_call(
        kernel,
        out_shape=shapes,
        in_specs=[vmem] * 4 + [hbm] * 3,
        out_specs=(hbm, hbm, hbm),
        scratch_shapes=[
            pltpu.VMEM((2, 16 * TOK, HALF), BF),
            pltpu.VMEM((2, 8 * BLK, 16 * TOK), BF),
            pltpu.VMEM((NZ, 16, 128), F32),
            pltpu.VMEM((2 * NZ, 16, 128), F32),
            pltpu.VMEM((8, 16 * TOK), F32),
            pltpu.VMEM((8, 16 * TOK), F32),
            pltpu.VMEM((2, 8 * BLK, HALF), BF),
            pltpu.VMEM((2, ROWS, D), BF),
            pltpu.VMEM((D, FF), BF),
            pltpu.VMEM((D, FF), BF),
            pltpu.VMEM((FF, D), BF),
            pltpu.VMEM((3, ROWS, FF), BF),
            pltpu.VMEM((2, 8 * BLK, HALF), BF),
            pltpu.VMEM((2, 2, 3, 128, HALF), BF),
            pltpu.VMEM((2, 2, 2, TOK, HALF), BF),
            pltpu.VMEM((NX, 3, 2, SHARE, HALF), BF),
            pltpu.VMEM((2, 3, 2, SHARE // 2, HALF), BF),
            pltpu.VMEM((2, 3, 2, SHARE, HALF), BF),
            pltpu.VMEM((2, TOK, HALF), BF),
            pltpu.VMEM((2, 2, TOK, HALF), BF),
            dma((3,)), dma((2, 2)), dma((2, 2)), dma((2,)), dma((2,)), dma((2,)),
            dma((NZ, 2)), dma((NZ, 2)),
            dma((len(OUT), 4, 2)), dma((len(OUT), 4, 2)),
            dma((len(OUT), 8)), dma((len(OUT), 8)),
            dma((len(BACK), 8)), dma((len(BACK), 8)),
            dma((len(BACK), 3, 2)), dma((len(BACK), 3, 2)),
            dma((len(BACK), 2, 2)), dma((len(BACK), 2, 2)),
            dma((2, 2 + NQ, 2)), dma((2, 2 + NQ, 2)),
            dma((len(BACK),)), dma((len(BACK),)), dma((10,)),
        ],
        compiler_params=pltpu.CompilerParams(
            collective_id=0, has_side_effects=True, vmem_limit_bytes=60 * 2**20
        ),
        cost_estimate=pl.CostEstimate(
            flops=30_000_000_000, bytes_accessed=20_000_000, transcendentals=450_000
        ),
        name="moe",
    )(tokens, cotangent, expert_ids.T, gates.T, w_gate[0], w_up[0], w_down[0])
    mixed, grad_tokens, grads = pl.pallas_call(
        place_outputs,
        out_shape=shapes,
        in_specs=[hbm] * 3,
        out_specs=(hbm, hbm, hbm),
        scratch_shapes=[
            pltpu.VMEM((TOK, D), BF),
            pltpu.VMEM((TOK, D), BF),
            pltpu.VMEM((3, SHARE, D), BF),
            dma((5,)), dma((5,)),
        ],
        name="place_outputs",
    )(*results)
    return mixed, grad_tokens, grads.transpose(1, 0, 2)[None]


def solution(mesh):
    return jax.shard_map(
        local,
        mesh=mesh,
        in_specs=(
            P(("dp", "expert"), None),
            P(("dp", "expert"), None),
            P(("dp", "expert"), None),
            P(("dp", "expert"), None),
            P("expert", None, None),
            P("expert", None, None),
            P("expert", None, None),
        ),
        out_specs=(
            P(("dp", "expert"), None),
            P(("dp", "expert"), None),
            P("expert", "dp", None, None),
        ),
        check_vma=False,
    )
```

```python
import jax
import jax.numpy as jnp
from jax import lax
from jax.experimental import pallas as pl
from jax.experimental.pallas import tpu as pltpu
from jax.sharding import PartitionSpec as P

MESH = pl.DeviceIdType.MESH
BF = jnp.bfloat16
F32 = jnp.float32

NX, NY, NZ = 4, 4, 8
D, FF, TOK, TOP, CAP = 2048, 768, 64, 8, 9
HALF = D // 2
BLK = 16 * CAP
ROWS = NY * BLK
SHARE = FF // NX
QC = 256
NQ = HALF // QC
FULL = [(n * QC, QC) for n in range(NQ)]
OUT = [(0, a, b) for a, b in [(0, 128), (128, 128)] + FULL[1:]] + [(1, a, b) for a, b in FULL]
BACK = [(0, a, b) for a, b in FULL] + [(1, a, b) for a, b in FULL[:-1] + [(768, 128), (896, 128)]]
NT = len(OUT) - NQ
WIDE = 512
ORDER = (2, 6, 4, 3, 7, 5, 1, 0)


def dot(a, b, ca, cb):
    return lax.dot_general(a, b, (((ca,), (cb,)), ((), ())), preferred_element_type=F32)


class Both:
    def __init__(self, *copies):
        self.copies = copies

    def start(self):
        for cp in self.copies:
            cp.start()

    def wait_recv(self):
        for cp in self.copies:
            cp.wait_recv()

    def wait_send(self):
        for cp in self.copies:
            cp.wait_send()


def kernel(
    tok, cot, ids, gates, wg_h, wu_h, wd_h,
    mixed_o, gtok_o, gw_o,
    T, S, meta_s, meta_r, pos, gat, yb, xin, wg, wu, wd, act, ret, zr, zl, G, xr1, xr2, tw, ob,
    w_sem, fs, fr, tws, twr, tls, ms, mr, zs, zrv, ys, yr, rs, rr, zbs, zbr, zls, zlr, xs, xrv,
    os_, orv, ol,
):
    x = lax.axis_index("dp")
    e = lax.axis_index("expert")
    y, z, c = e // 16, lax.rem(e // 2, NZ), lax.rem(e, 2)

    def at(dx, dy, dz, dc):
        return (
            lax.rem(x + dx + NX, NX),
            (lax.rem(y + dy + NY, NY) * NZ + lax.rem(z + dz + NZ, NZ)) * 2 + lax.rem(c + dc, 2),
        )

    def remote(src, dst, ssem, rsem, where):
        return pltpu.make_async_remote_copy(
            src_ref=src, dst_ref=dst, send_sem=ssem, recv_sem=rsem,
            device_id=where, device_id_type=MESH,
        )

    w_in = [
        pltpu.make_async_copy(src, dst, w_sem.at[i])
        for i, (src, dst) in enumerate(((wg_h, wg), (wu_h, wu), (wd_h, wd)))
    ]
    for cp in w_in:
        cp.start()

    idv = ids[...]
    place = ((idv >> 1) & 7) * 8 + (idv >> 4) * 2 + (idv & 1)
    row = lax.broadcasted_iota(jnp.int32, (64, TOK), 0)
    named = jnp.zeros((64, TOK), F32)
    gated = jnp.zeros((64, TOK), F32)
    for k in range(TOP):
        hit = place[k : k + 1, :] == row
        named = named + jnp.where(hit, 1.0, 0.0)
        gated = gated + jnp.where(hit, gates[k : k + 1, :], 0.0)
    t0 = lax.broadcasted_iota(jnp.int32, (TOK, 128), 0)
    l0 = lax.broadcasted_iota(jnp.int32, (TOK, 128), 1) - TOK * c
    same = jnp.where(t0 == l0, 1.0, 0.0).astype(BF)
    upto = jnp.where(t0 <= l0, jnp.where(l0 < TOK, 1.0, 0.0), 0.0).astype(BF)
    named = named.astype(BF)
    rank = dot(named, upto, 1, 0) * dot(named, same, 1, 0)
    gate_t = dot(gated.astype(BF), same, 1, 0)
    for k in range(NZ):
        meta_s[k, 0:8, :] = rank[k * 8 : k * 8 + 8]
        meta_s[k, 8:16, :] = gate_t[k * 8 : k * 8 + 8]

    greet = [(0, 0, dz, dc) for dz in range(NZ) for dc in range(2) if dz or dc]
    greet += [(0, dy, 0, dc) for dy in range(1, NY) for dc in range(2)]
    greet += [(1, 0, 0, 0), (-1, 0, 0, 0)]
    bar = pltpu.get_barrier_semaphore()
    for g in greet:
        pl.semaphore_signal(bar, inc=1, device_id=at(*g), device_id_type=MESH)
    pl.semaphore_wait(bar, len(greet))

    def zrow(dz, lo=0, n=128):
        return pl.ds(pl.multiple_of(lax.rem(z + dz + NZ, NZ) * 128 + lo, 16), n)

    mine = pl.ds(pl.multiple_of(c * HALF, HALF), HALF)
    other = pl.ds(pl.multiple_of((1 - c) * HALF, HALF), HALF)

    my_slot = pl.ds(pl.multiple_of(z * 128 + c * TOK, TOK), TOK)

    def first(way):
        i = 0 if way == 1 else 1
        _, lo, n = OUT[0]
        return Both(*(
            remote(
                tok.at[:, pl.ds(pl.multiple_of(lax.rem(c + dc, 2) * HALF + lo, 128), n)],
                T.at[0, my_slot, pl.ds(lo, n)], fs.at[i, dc], fr.at[i, dc], at(0, 0, way, dc),
            )
            for dc in range(2)
        ))

    begin = {w: first(w) for w in (1, -1)}
    for w in (1, -1):
        begin[w].start()
    swaps, keeps = [], []
    for a, src in enumerate((tok, cot)):
        cp = remote(src.at[:, other], T.at[a, my_slot, :], tws.at[a], twr.at[a], at(0, 0, 0, 1))
        cp.start()
        swaps.append(cp)
        cp = pltpu.make_async_copy(src.at[:, mine], T.at[a, my_slot, :], tls.at[a])
        cp.start()
        keeps.append(cp)

    metas = []
    for dz in (1, 7, 2, 6, 3, 5, 4, 0):
        for dc in (0, 1):
            src = meta_s.at[lax.rem(z + dz, NZ)]
            dst = meta_r.at[z * 2 + c]
            if dz == 0 and dc == 0:
                cp = pltpu.make_async_copy(src, dst, mr.at[0, 0])
            else:
                cp = remote(src, dst, ms.at[dz, dc], mr.at[dz, dc], at(0, 0, dz, dc))
            cp.start()
            metas.append((cp, dz or dc))

    NP = len(OUT)

    def zcopy(p, s, way):
        if p == 0 and s == 0:
            return begin[way]
        a, lo, n = OUT[p]
        cols = pl.ds(lo, n)
        rows = zrow(-s * way) if s < 3 else zrow(-3 * way, 0 if way == 1 else 64, 64)
        i = 0 if way == 1 else 1
        return remote(
            T.at[a, rows, cols], T.at[a, rows, cols],
            zs.at[p, s, i], zrv.at[p, s, i], at(0, 0, way, 0),
        )

    zc = {(p, s, w): zcopy(p, s, w) for p in range(NP) for s in range(4) for w in (1, -1)}

    def zstart(p, s):
        for w in (1, -1):
            if s:
                zc[p, s - 1, w].wait_recv()
            zc[p, s, w].start()

    def target(r):
        return at(0, r // 2, 0, r % 2)

    my_rows = pl.ds(pl.multiple_of(y * BLK, 16), BLK)

    def ycopy(p, r):
        a, lo, n = OUT[p]
        src = yb.at[a, pl.ds(r * BLK, BLK), pl.ds(lo, n)]
        dst = xin.at[a, my_rows, pl.ds(pl.multiple_of(c * HALF + lo, 128), n)]
        if r == 0:
            return pltpu.make_async_copy(src, dst, yr.at[p, 0])
        return remote(src, dst, ys.at[p, r], yr.at[p, r], target(r))

    yc = {(p, r): ycopy(p, r) for p in range(NP) for r in range(8)}

    def select(p, dy):
        a, lo, n = OUT[p]
        block = slice(2 * dy * BLK, 2 * (dy + 1) * BLK)
        cols = slice(lo, lo + n)
        yb[a, block, cols] = dot(S[a, block, :], T[a, :, cols], 1, 0).astype(BF)
        yc[p, 2 * dy + 1].start()
        yc[p, 2 * dy].start()

    for a in range(2):
        swaps[a].wait_recv()
        keeps[a].wait()
    zstart(1, 0)
    zstart(0, 1)

    def places():
        for cp, far in metas:
            if far:
                cp.wait_recv()
            else:
                cp.wait()
        lane8 = lax.broadcasted_iota(jnp.int32, (8, 128), 1)
        for k in range(NZ):
            enc = meta_r[2 * k, 0:8, :] + meta_r[2 * k + 1, 0:8, :]
            base = jnp.where(lane8 < TOK, 2.0 * k * CAP - 1.0, (2.0 * k + 1.0) * CAP - 1.0)
            pos[:, k * 128 : (k + 1) * 128] = jnp.where(enc > 0.5, enc + base, -1.0)
            gat[:, k * 128 : (k + 1) * 128] = meta_r[2 * k, 8:16, :] + meta_r[2 * k + 1, 8:16, :]

    def build(r, carry):
        row16 = lax.broadcasted_iota(jnp.int32, (16, 16 * TOK), 0).astype(F32)
        j = lax.rem(y + r // 2, NY) * 2 + lax.rem(c + r, 2)
        prow = pos[pl.ds(j, 1), :]
        grow = gat[pl.ds(j, 1), :]
        for i in range(BLK // 16):
            hit = row16 + float(16 * i) == prow
            at_rows = pl.ds(pl.multiple_of(r * BLK + 16 * i, 16), 16)
            S[0, at_rows, :] = jnp.where(hit, 1.0, 0.0).astype(BF)
            S[1, at_rows, :] = jnp.where(hit, grow, 0.0).astype(BF)
        return carry

    def arrived(p):
        for r in range(8):
            if r:
                yc[p, r].wait_recv()
                yc[p, r].wait_send()
            else:
                yc[p, r].wait()

    HR = ROWS // 2

    def forward(n):
        def part(i, carry):
            rows = pl.ds(pl.multiple_of(i * HR, 16), HR)
            cols = slice(n * 256, (n + 1) * 256)
            v = xin[0, rows, :]
            g = dot(v, wg[:, cols], 1, 0)
            u = dot(v, wu[:, cols], 1, 0)
            sg = jax.nn.sigmoid(g)
            silu = g * sg
            act[0, rows, cols] = (silu * u).astype(BF)
            act[1, rows, cols] = (u * sg * (1.0 + g * (1.0 - sg))).astype(BF)
            act[2, rows, cols] = silu.astype(BF)
            return carry

        lax.fori_loop(0, 2, part, 0)

    DY = (1, 3, 2, 0)
    for t in range(2, NP + 4):
        if t >= 4:
            for w in (1, -1):
                zc[t - 4, 3, w].wait_recv()
        for i in range(4):
            k = t - 3 + i
            if t >= 4:
                select(t - 4, DY[i])
            if 0 <= k < NP:
                zstart(k, t - k)
        if t == 2:
            places()
        if t == 3:
            lax.fori_loop(0, 8, build, 0)

    for p in range(NT):
        arrived(p)
    for cp in w_in:
        cp.wait()
    for n in range(FF // 256):
        forward(n)

    def give_back(a, q, h, rows):
        for k in range(NY):
            r = lax.rem(k - y + NY, NY) * 2 + lax.rem(h - c + 2, 2)
            yb[a, pl.ds(pl.multiple_of(r * BLK, 16), BLK), q * WIDE : (q + 1) * WIDE] = (
                rows[k * BLK : (k + 1) * BLK].astype(BF)
            )

    def rcopy(k, r):
        a, lo, n = BACK[k]
        cols = pl.ds(lo, n)
        there = (NY - r // 2) % NY * 2 + r % 2
        src = yb.at[a, pl.ds(r * BLK, BLK), cols]
        dst = ret.at[a, pl.ds(there * BLK, BLK), cols]
        if r == 0:
            return pltpu.make_async_copy(src, dst, rr.at[k, 0])
        return remote(src, dst, rs.at[k, r], rr.at[k, r], target(r))

    NB = len(BACK)
    rc = {(k, r): rcopy(k, r) for k in range(NB) for r in range(8)}

    def send_back(a, q):
        for k in range(NB):
            if BACK[k][0] == a and BACK[k][1] // WIDE == q:
                for r in ORDER:
                    rc[k, r].start()

    def results(q):
        for h in range(2):
            n = h * HALF + q * WIDE
            give_back(0, q, h, dot(act[0], wd[:, n : n + WIDE], 1, 0))
        send_back(0, q)

    def xshare(dx):
        return lax.rem(x + dx + NX, NX)

    SH2 = SHARE // 2

    def piece(n):
        if n < 2:
            return n, slice(0, HALF)
        return 2, slice((n - 2) * QC, (n - 1) * QC)

    PIECES = 2 + NQ

    def xcopy1(n, way):
        i = 0 if way == 1 else 1
        m, cols = piece(n)
        return remote(
            G.at[xshare(2), m, :, pl.ds(i * SH2, SH2), cols], xr1.at[i, m, :, :, cols],
            xs.at[0, n, i], xrv.at[0, n, i], at(way, 0, 0, 0),
        )

    def xcopy2(n, way):
        i = 0 if way == 1 else 1
        m, cols = piece(n)
        return remote(
            G.at[xshare(way), m, :, :, cols], xr2.at[i, m, :, :, cols],
            xs.at[1, n, i], xrv.at[1, n, i], at(way, 0, 0, 0),
        )

    xc1 = {(n, w): xcopy1(n, w) for n in range(PIECES) for w in (1, -1)}
    xc2 = {(n, w): xcopy2(n, w) for n in range(PIECES) for w in (1, -1)}

    def product(m, b, k, h, cols, at_cols):
        for hf in range(2):
            v = dot(act[k, :, hf * 384 : (hf + 1) * 384], xin[b, :, cols], 0, 0).astype(BF)
            G[2 * hf, m, h, :, at_cols] = v[:SHARE]
            G[2 * hf + 1, m, h, :, at_cols] = v[SHARE:]

    def weights(m, b, k):
        def part(i, carry):
            here = pl.ds(pl.multiple_of(i * WIDE, WIDE), WIDE)
            for h in range(2):
                cols = pl.ds(pl.multiple_of(h * HALF + i * WIDE, WIDE), WIDE)
                product(m, b, k, h, cols, here)
            return carry

        lax.fori_loop(0, HALF // WIDE, part, 0)
        for w in (1, -1):
            xc1[m, w].start()

    def xadd(n):
        m, cols = piece(n)
        for i, w in enumerate((1, -1)):
            xc1[n, w].wait_recv()
            rows = pl.ds(i * SH2, SH2)
            d = xshare(w)
            for h in range(2):
                G[d, m, h, rows, cols] = (
                    G[d, m, h, rows, cols].astype(F32) + xr1[i, m, h, :, cols].astype(F32)
                ).astype(BF)
            xc2[n, w].start()

    def xfinish(m):
        for n in range(PIECES):
            if piece(n)[0] == m:
                for w in (1, -1):
                    xc2[n, w].wait_recv()
        own = xshare(0)
        for h in range(2):
            G[own, m, h] = (
                G[own, m, h].astype(F32) + xr2[0, m, h].astype(F32) + xr2[1, m, h].astype(F32)
            ).astype(BF)
            cp = pltpu.make_async_copy(
                G.at[own, m, h], gw_o.at[m, :, pl.ds(h * HALF, HALF)], ol.at[4 + 2 * m + h]
            )
            cp.start()
            tail.append(cp)

    tail = []
    for i in range(NQ):
        arrived(NT + i)
        for h in range(2):
            n = h * HALF + i * QC
            product(2, 1, 0, h, slice(n, n + QC), slice(i * QC, (i + 1) * QC))
        for w in (1, -1):
            xc1[2 + i, w].start()
        if i < HALF // WIDE:
            results(i)
        if i > 1:
            xadd(i)

    def backward(i, carry):
        cols = pl.ds(pl.multiple_of(i * 256, 256), 256)
        g = dot(xin[1], wd[cols, :], 1, 1)
        act[1, :, cols] = (g * act[1, :, cols].astype(F32)).astype(BF)
        act[2, :, cols] = (g * act[2, :, cols].astype(F32)).astype(BF)
        return carry

    for a in range(2):
        swaps[a].wait_send()
    for key in zc:
        zc[key].wait_send()

    own_rows = {0: my_slot, 1: pl.ds(pl.multiple_of(z * 128 + (1 - c) * TOK, TOK), TOK)}

    def bcopy(k, s, way):
        a, lo, n = BACK[k]
        i = 0 if way == 1 else 1
        cols = pl.ds(lo, n)
        if s == 3:
            return Both(*(
                remote(
                    T.at[a, zrow(way, lax.rem(c + dc, 2) * TOK, TOK), cols],
                    zl.at[a, i, c, :, cols], zls.at[k, i, dc], zlr.at[k, i, dc],
                    at(0, 0, way, dc),
                )
                for dc in range(2)
            ))
        rows = zrow((4 - s) * way) if s else zrow(4, 64 * i, 64)
        dst = zr.at[a, i, s, :, cols] if s else zr.at[a, i, 0, pl.ds(0, 64), cols]
        return remote(
            T.at[a, rows, cols], dst, zbs.at[k, s, i], zbr.at[k, s, i], at(0, 0, way, 0)
        )

    def tcopy(k):
        a, lo, n = BACK[k]
        cols = pl.ds(lo, n)
        return remote(
            T.at[a, own_rows[1], cols], tw.at[a, :, cols], os_.at[k], orv.at[k], at(0, 0, 0, 1)
        )

    bc = {(k, s, w): bcopy(k, s, w) for k in range(NB) for s in range(4) for w in (1, -1)}
    tc = {(k,): tcopy(k) for k in range(NB)}

    def combine(k):
        a, lo, n = BACK[k]
        for r in range(8):
            if r:
                rc[k, r].wait_recv()
            else:
                rc[k, r].wait()
        cols = slice(lo, lo + n)
        for j in range(2):
            half = slice(j * 512, (j + 1) * 512)
            T[a, half, cols] = dot(S[1 - a, :, half], ret[a, :, cols], 0, 0).astype(BF)
        for w in (1, -1):
            bc[k, 0, w].start()
        tc[k,].start()

    def pass_on(k, s):
        a, lo, n = BACK[k]
        cols = slice(lo, lo + n)
        for i, w in enumerate((1, -1)):
            bc[k, s - 1, w].wait_recv()
            m = 64 if s == 1 else 128
            rows = zrow((4 - s) * w, 64 * i if s == 1 else 0, m)
            T[a, rows, cols] = (
                T[a, rows, cols].astype(F32) + zr[a, i, s - 1, 0:m, cols].astype(F32)
            ).astype(BF)
            bc[k, s, w].start()

    def finish(k):
        a, lo, n = BACK[k]
        cols = slice(lo, lo + n)
        for w in (1, -1):
            bc[k, 3, w].wait_recv()
        tc[k,].wait_recv()
        for h, mid in ((c, T[a, own_rows[0], cols]), (1 - c, tw[a, :, cols])):
            ob[a, h, :, cols] = (
                mid.astype(F32)
                + zl[a, 0, h, :, cols].astype(F32)
                + zl[a, 1, h, :, cols].astype(F32)
            ).astype(BF)

    outs = (mixed_o, gtok_o)

    def deliver(a):
        for h in range(2):
            cp = pltpu.make_async_copy(
                ob.at[a, h], outs[a].at[:, pl.ds(h * HALF, HALF)], ol.at[2 * a + h]
            )
            cp.start()
            tail.append(cp)

    def slot_grads(q):
        for h in range(2):
            n = h * HALF + q * WIDE
            give_back(
                1, q, h,
                dot(act[1], wg[n : n + WIDE, :], 1, 1) + dot(act[2], wu[n : n + WIDE, :], 1, 1),
            )
        send_back(1, q)

    lax.fori_loop(0, FF // 256, backward, 0)
    weights(0, 0, 1)
    xadd(NQ)
    xadd(1 + NQ)
    between = {
        0: lambda: (weights(1, 0, 2), slot_grads(0)),
        1: lambda: slot_grads(1),
        3: lambda: xadd(0),
        4: lambda: xadd(1),
        NB - 2: lambda: xfinish(2),
        NB + 2: lambda: xfinish(0),
    }
    for t in range(NB + 4):
        for k in range(max(0, t - 4), min(t, NB)):
            if t - k < 4:
                pass_on(k, t - k)
            else:
                finish(k)
                if k == NQ - 1:
                    deliver(0)
        if t < NB:
            combine(t)
        if t in between:
            between[t]()
    deliver(1)
    xfinish(1)

    for cp, far in metas:
        if far:
            cp.wait_send()
    for key in rc:
        if key[1]:
            rc[key].wait_send()
    for key in tc:
        tc[key].wait_send()
    for key in bc:
        bc[key].wait_send()
    for key in xc1:
        xc1[key].wait_send()
        xc2[key].wait_send()
    for cp in tail:
        cp.wait()


def place_outputs(a, b, g, a_o, b_o, g_o, va, vb, vg, s_in, s_out):
    moves = [(g.at[m], vg.at[m], g_o.at[m]) for m in range(3)] + [(a, va, a_o), (b, vb, b_o)]
    into = [pltpu.make_async_copy(u, v, s_in.at[i]) for i, (u, v, _) in enumerate(moves)]
    out = [pltpu.make_async_copy(v, w, s_out.at[i]) for i, (_, v, w) in enumerate(moves)]
    for cp in into:
        cp.start()
    for cp, nxt in zip(into, out):
        cp.wait()
        nxt.start()
    for cp in out:
        cp.wait()


def local(tokens, expert_ids, gates, cotangent, w_gate, w_up, w_down):
    vmem = pl.BlockSpec(memory_space=pltpu.VMEM)
    hbm = pl.BlockSpec(memory_space=pl.ANY)
    dma = pltpu.SemaphoreType.DMA
    shapes = (
        jax.ShapeDtypeStruct((TOK, D), BF),
        jax.ShapeDtypeStruct((TOK, D), BF),
        jax.ShapeDtypeStruct((3, SHARE, D), BF),
    )
    results = pl.pallas_call(
        kernel,
        out_shape=shapes,
        in_specs=[vmem] * 4 + [hbm] * 3,
        out_specs=(hbm, hbm, hbm),
        scratch_shapes=[
            pltpu.VMEM((2, 16 * TOK, HALF), BF),
            pltpu.VMEM((2, 8 * BLK, 16 * TOK), BF),
            pltpu.VMEM((NZ, 16, 128), F32),
            pltpu.VMEM((2 * NZ, 16, 128), F32),
            pltpu.VMEM((8, 16 * TOK), F32),
            pltpu.VMEM((8, 16 * TOK), F32),
            pltpu.VMEM((2, 8 * BLK, HALF), BF),
            pltpu.VMEM((2, ROWS, D), BF),
            pltpu.VMEM((D, FF), BF),
            pltpu.VMEM((D, FF), BF),
            pltpu.VMEM((FF, D), BF),
            pltpu.VMEM((3, ROWS, FF), BF),
            pltpu.VMEM((2, 8 * BLK, HALF), BF),
            pltpu.VMEM((2, 2, 3, 128, HALF), BF),
            pltpu.VMEM((2, 2, 2, TOK, HALF), BF),
            pltpu.VMEM((NX, 3, 2, SHARE, HALF), BF),
            pltpu.VMEM((2, 3, 2, SHARE // 2, HALF), BF),
            pltpu.VMEM((2, 3, 2, SHARE, HALF), BF),
            pltpu.VMEM((2, TOK, HALF), BF),
            pltpu.VMEM((2, 2, TOK, HALF), BF),
            dma((3,)), dma((2, 2)), dma((2, 2)), dma((2,)), dma((2,)), dma((2,)),
            dma((NZ, 2)), dma((NZ, 2)),
            dma((len(OUT), 4, 2)), dma((len(OUT), 4, 2)),
            dma((len(OUT), 8)), dma((len(OUT), 8)),
            dma((len(BACK), 8)), dma((len(BACK), 8)),
            dma((len(BACK), 3, 2)), dma((len(BACK), 3, 2)),
            dma((len(BACK), 2, 2)), dma((len(BACK), 2, 2)),
            dma((2, 2 + NQ, 2)), dma((2, 2 + NQ, 2)),
            dma((len(BACK),)), dma((len(BACK),)), dma((10,)),
        ],
        compiler_params=pltpu.CompilerParams(
            collective_id=0, has_side_effects=True, vmem_limit_bytes=60 * 2**20
        ),
        cost_estimate=pl.CostEstimate(
            flops=30_000_000_000, bytes_accessed=20_000_000, transcendentals=450_000
        ),
        name="moe",
    )(tokens, cotangent, expert_ids.T, gates.T, w_gate[0], w_up[0], w_down[0])
    mixed, grad_tokens, grads = pl.pallas_call(
        place_outputs,
        out_shape=shapes,
        in_specs=[hbm] * 3,
        out_specs=(hbm, hbm, hbm),
        scratch_shapes=[
            pltpu.VMEM((TOK, D), BF),
            pltpu.VMEM((TOK, D), BF),
            pltpu.VMEM((3, SHARE, D), BF),
            dma((5,)), dma((5,)),
        ],
        name="place_outputs",
    )(*results)
    return mixed, grad_tokens, grads.transpose(1, 0, 2)[None]


def solution(mesh):
    return jax.shard_map(
        local,
        mesh=mesh,
        in_specs=(
            P(("dp", "expert"), None),
            P(("dp", "expert"), None),
            P(("dp", "expert"), None),
            P(("dp", "expert"), None),
            P("expert", None, None),
            P("expert", None, None),
            P("expert", None, None),
        ),
        out_specs=(
            P(("dp", "expert"), None),
            P(("dp", "expert"), None),
            P("expert", "dp", None, None),
        ),
        check_vma=False,
    )
```
